128 devices in a mesh: dp: 32 (over y, x, core), mp: 4 (over z).
Axes of the slice: x: 4, y: 4, z: 4, core: 2. Of those that a mesh axis runs over, the one named last changes fastest.
Arguments:
- acts: bfloat16 [8, 4096, 1024], P(None, 'dp')
- grads_out: bfloat16 [8, 4096, 16384], P(None, 'dp', 'mp')
- counts: int32 [32], replicated, may hold values from 64 to 128, as said below
- owners: int32 [32], replicated, may hold values from 0 to 31, each once
- bases_a: bfloat16 [8, 1024, 1024], P(None, 'mp'), may hold values from -0.1875 to 0.1875
- bases_g: bfloat16 [4, 32, 1024, 1024], P('mp', 'dp'), may hold values from -0.1875 to 0.1875
Outputs:
- precond: bfloat16 [8, 16, 1024, 1024], P(None, 'mp', 'dp')
The draws below stay inside these ranges and needn't reach their ends.
Inputs may be any that keep to these rules, and one draw needn't show every extreme that they name: `owners`: every dp index owns exactly one of the 32 block positions. Rows of shard s at positions counts[s] and beyond are padding.
All inputs are finite; a program needn't handle non-finite values.
Results may differ from the reference program's by a relative error of at most 0.0065.
Values may be sent and summed in bfloat16 or wider, within the bound.
A program may use at most 128 MiB of HBM per device.

```python
import jax
import jax.numpy as jnp
from jax import lax

BLK = 1024
NGM = 4
TOK_DEV = 128
LAY = 8
TOKENS = 4096
N_DP = 32
N_MP = 4


def draw_acts(key, part):
    key = jax.random.fold_in(key, 11)
    key_list = jax.random.split(key, 3)
    row_scale = 10.0 ** jax.random.uniform(key_list[0], (LAY, TOKENS, 1)) / 4.64
    col_scale = 10.0 ** jax.random.uniform(key_list[1], (LAY, 1, BLK)) / 4.64
    values = jax.random.normal(key_list[2], (LAY, TOKENS, BLK))
    return (values * row_scale * col_scale).astype(jnp.bfloat16)


def draw_grads_out(key, part):
    key = jax.random.fold_in(key, 13)
    key_list = jax.random.split(key, 3)
    width_all = NGM * N_MP * BLK
    row_scale = 10.0 ** jax.random.uniform(key_list[0], (LAY, TOKENS, 1)) / 4.64
    col_scale = 10.0 ** jax.random.uniform(key_list[1], (LAY, 1, width_all)) / 4.64
    values = jax.random.normal(key_list[2], (LAY, TOKENS, width_all))
    return (values * row_scale * col_scale / 64.0).astype(jnp.bfloat16)


def draw_counts(key, part):
    key = jax.random.fold_in(key, 5)
    first_key, second_key = jax.random.split(key)
    values = jax.random.randint(first_key, (N_DP,), TOK_DEV // 2, TOK_DEV + 1)
    order = jax.random.permutation(second_key, N_DP)
    values = values.at[order[0]].set(TOK_DEV).at[order[1]].set(TOK_DEV // 2)
    return values.astype(jnp.int32)


def levels(stream_key, shape, cuts, least, largest):
    gain, own = 1.0, jax.random.fold_in(stream_key, 6)
    for position, shards_of in cuts:
        draws = jnp.exp(jax.random.uniform(jax.random.fold_in(own, position), (shards_of,), jnp.float32, least / len(cuts), largest / len(cuts)))
        gain = gain * jnp.repeat(draws, shape[position] // shards_of).reshape([-1 if axis == position else 1 for axis in range(len(shape))])
    return gain


def scatter_about(own_key, dims, scale, reach, cuts=(), kind=jnp.bfloat16):
    array = scale * jax.random.normal(own_key, dims, jnp.float32)
    if cuts:
        array = array * levels(own_key, dims, cuts, -0.22, 0.18)
    return jnp.clip(array, -reach, reach).astype(kind)


def setup_inputs(seed: int = 0) -> dict:
    splits = jax.random.split(jax.random.key(seed), 7)
    acts = draw_acts(jax.random.fold_in(splits[6], 71), 0)
    grads_out = draw_grads_out(jax.random.fold_in(splits[6], 71), 0)
    counts = draw_counts(jax.random.fold_in(splits[6], 71), 0)
    owners = jax.random.permutation(splits[3], N_DP).astype(jnp.int32)
    bases_a = scatter_about(splits[4], (LAY, BLK, BLK), BLK ** -0.5, 0.1875, ((1, 4),))
    bases_g = scatter_about(splits[5], (N_MP, N_DP, BLK, BLK), BLK ** -0.5, 0.1875, ((0, 4), (1, 32)))
    return dict(acts=acts, grads_out=grads_out, counts=counts, owners=owners, bases_a=bases_a, bases_g=bases_g)


damping = 1e-4


def reference(acts, grads_out, counts, owners, bases_a, bases_g):
    row_ids = jnp.arange(TOKENS, dtype=jnp.int32)
    shard_of = row_ids // TOK_DEV
    live_rows = (row_ids % TOK_DEV) < counts[shard_of]
    row_total = jnp.sum(counts).astype(jnp.float32)
    zero_value = jnp.zeros((), jnp.bfloat16)
    masked_acts = jnp.where(live_rows[None, :, None], acts, zero_value)
    masked_grads = jnp.where(live_rows[None, :, None], grads_out, zero_value)
    layers_out = []
    for layer_index in range(LAY):
        basis_a = bases_a[layer_index]
        proj_a = jnp.dot(masked_acts[layer_index], basis_a, preferred_element_type=jnp.float32)
        lam_a = jnp.sum(proj_a * proj_a, axis=0) / row_total
        proj_a16 = proj_a.astype(jnp.bfloat16)
        blocks_out = []
        for column_index in range(NGM * N_MP):
            group_index = column_index // NGM
            unit_index = layer_index * NGM + column_index % NGM
            owner_index = owners[unit_index]
            basis_g = bases_g[group_index, owner_index]
            rows_g = masked_grads[layer_index, :, column_index * BLK:(column_index + 1) * BLK]
            proj_g = jnp.dot(rows_g, basis_g, preferred_element_type=jnp.float32)
            lam_g = jnp.sum(proj_g * proj_g, axis=0) / row_total
            cross = lax.dot_general(proj_a16, proj_g.astype(jnp.bfloat16), (((0,), (0,)), ((), ())), preferred_element_type=jnp.float32) / row_total
            scaled = (cross / (lam_a[:, None] * lam_g[None, :] + damping)).astype(jnp.bfloat16)
            right = lax.dot_general(scaled, basis_g, (((1,), (1,)), ((), ())), preferred_element_type=jnp.float32).astype(jnp.bfloat16)
            blocks_out.append(jnp.dot(basis_a, right, preferred_element_type=jnp.float32).astype(jnp.bfloat16))
        layers_out.append(jnp.stack(blocks_out))
    return jnp.stack(layers_out)
```

```python
import functools

import jax
import jax.numpy as jnp
from jax import lax
from jax.experimental import pallas as pl
from jax.experimental.pallas import tpu as pltpu
from jax.sharding import PartitionSpec as P

MESH = pl.DeviceIdType.MESH
damping = 0.0001
BLK = 1024
TILE = 256
NY, NX, NC, NZ = 4, 4, 2, 4
N_DP = NY * NX * NC
HALF = 64
SUB = HALF // NZ

PAIRS = [(2, 2), (1, 3), (3, 1), (2, 0), (0, 2), (1, 1), (3, 3), (2, 1), (2, 3), (1, 2), (3, 2), (0, 1), (1, 0), (0, 3), (3, 0)]
SPREAD = [(dy, dx, dc) for dc in range(NC) for dy, dx in PAIRS] + [(0, 0, 1)]
SLOTS = (1, 3, 2)


def kernel(
    inv_ref, own_ref, cnt_ref, acts_hbm, grads_hbm, ba_hbm, bg_hbm, out_hbm,
    graw, araw, baraw, bg, first, mid, rows, sa, ra, proj, basis, lam, lam_a, lam_g, cross, back, mask,
    load_sem, act_send, act_recv, ba_send, ba_recv, lam_send, lam_recv,
    p1_send, p1_recv, p1e_send, p1e_recv, p2_send, p2_recv, z_send, z_recv, zf_send, zf_recv, out_send, out_recv, store_sem,
):
    me, mz = lax.axis_index("dp"), lax.axis_index("mp")
    my, mx, mc = me // 8, (me // 2) % 4, me % 2

    def at(dy, dx, dc):
        return ((my + dy) % NY) * 8 + ((mx + dx) % NX) * 2 + (mc + dc) % NC

    def zat(dz):
        return (me, (mz + dz) % NZ)

    def send(src, dst, ssem, rsem, target):
        copy = pltpu.make_async_remote_copy(
            src_ref=src, dst_ref=dst, send_sem=ssem, recv_sem=rsem, device_id=target, device_id_type=MESH
        )
        copy.start()
        return copy

    loads = [
        pltpu.make_async_copy(acts_hbm.at[:, pl.ds(mz * SUB, SUB)], araw.at[:, 0], load_sem.at[0]),
        pltpu.make_async_copy(acts_hbm.at[:, pl.ds(HALF + mz * SUB, SUB)], araw.at[:, 1], load_sem.at[1]),
        pltpu.make_async_copy(ba_hbm, baraw, load_sem.at[2]),
    ]
    for j in range(4):
        loads.append(
            pltpu.make_async_copy(grads_hbm.at[:, :, pl.ds(j * BLK, BLK)], graw.at[:, j], load_sem.at[3 + j])
        )
    loads.append(pltpu.make_async_copy(bg_hbm, bg, load_sem.at[7]))
    for copy in loads:
        copy.start()

    barrier = pltpu.get_barrier_semaphore()
    peers = [(at(*d), mz) for d in SPREAD] + [zat(dz) for dz in (1, 2, 3)]
    for peer in peers:
        pl.semaphore_signal(barrier, inc=1, device_id=peer, device_id_type=MESH)

    live = cnt_ref[me] - HALF
    row_ids = lax.broadcasted_iota(jnp.int32, (HALF, BLK), 0)
    mask[...] = jnp.where(row_ids < live, 1.0, 0.0).astype(jnp.bfloat16)

    loads[0].wait()
    loads[1].wait()
    pl.semaphore_wait(barrier, len(peers))

    sub_mask = mask[pl.ds(pl.multiple_of(mz * SUB, SUB), SUB), :]

    def pack_acts(dst, index, disp):
        layer = inv_ref[at(*disp)] // 4
        dst[index, pl.ds(0, SUB), :] = araw[layer, 0]
        dst[index, pl.ds(SUB, SUB), :] = araw[layer, 1] * sub_mask

    def index_of(dy, dx, dc):
        return (dy * 4 + dx) * 2 + dc

    act_copies = []
    for disp in SPREAD:
        i = index_of(*disp)
        pack_acts(sa, i, disp)
        act_copies.append(send(sa.at[i], ra.at[i], act_send.at[i], act_recv.at[i], (at(*disp), mz)))
    pack_acts(ra, 0, (0, 0, 0))

    loads[2].wait()
    basis[mz] = baraw[inv_ref[me] // 4]
    ba_copies = [
        send(basis.at[mz], basis.at[mz], ba_send.at[k], ba_recv.at[k], zat(dz)) for k, dz in enumerate(SLOTS)
    ]

    for j in range(4):
        loads[3 + j].wait()

    def disp_of(half, slot, e):
        other, dc = e // 2, e % 2
        return (other, slot, dc) if half == 0 else (slot, other, dc)

    def hop(half, slot):
        return (at(0, slot, 0) if half == 0 else at(slot, 0, 0), mz)

    def pack(half, disp):
        unit = inv_ref[at(*disp)]
        block = graw[unit // 4, unit % 4, pl.ds(half * HALF, HALF), :]
        return block if half == 0 else block * mask[...]

    p1, p1e, p2 = {}, {}, {}
    for slot in SLOTS:
        for half in range(2):
            for e in range(8):
                first[half, slot - 1, e] = pack(half, disp_of(half, slot, e))
            p1[half, slot] = send(
                first.at[half, slot - 1, pl.ds(1, 7)], mid.at[half, slot],
                p1_send.at[half, slot], p1_recv.at[half, slot], hop(half, slot),
            )
            p1e[half, slot] = send(
                first.at[half, slot - 1, 0], rows.at[(half * 4 + slot) * 8],
                p1e_send.at[half, slot], p1e_recv.at[half, slot], hop(half, slot),
            )

    def forward(half, slot):
        for e in (4, 5, 2, 6, 3, 7, 1):
            disp = (e // 2, 0, e % 2) if half == 0 else (0, e // 2, e % 2)
            p2[half, slot, e] = send(
                mid.at[half, slot, e - 1], rows.at[(half * 4 + slot) * 8 + e],
                p2_send.at[half, slot, e], p2_recv.at[half, slot, e], (at(*disp), mz),
            )

    for half in range(2):
        for e in range(1, 8):
            mid[half, 0, e - 1] = pack(half, disp_of(half, 0, e))
        rows[half * 32] = pack(half, disp_of(half, 0, 0))
        forward(half, 0)

    for copy in act_copies:
        copy.wait_recv()
    for copy in ba_copies:
        copy.wait_recv()
    lam[mz] = jnp.zeros((8, BLK), jnp.float32)

    def proj_a_step(step, carry):
        dy, cols = step // 4, pl.ds(pl.multiple_of((step % 4) * TILE, TILE), TILE)
        block = ra[pl.ds(dy * 8, 8)].reshape(256, BLK)
        value = jnp.dot(
            block, basis[:, :, cols].reshape(BLK, TILE), preferred_element_type=jnp.float32
        )
        lam[mz, :, cols] += jnp.sum((value * value).reshape(32, 8, TILE), axis=0)
        value = value.astype(jnp.bfloat16)
        for dx in range(4):
            for dc in range(2):
                r = (dx * 2 + dc) * 32
                proj[dx * 8 + dy * 2 + dc, mz, :, cols] = value[r : r + SUB]
                proj[(4 + dy) * 8 + dx * 2 + dc, mz, :, cols] = value[r + SUB : r + 2 * SUB]
        return carry

    lax.fori_loop(0, 16, proj_a_step, 0)

    z_copies = {}
    for k, dz in enumerate((1, 3)):
        z_copies[dz] = send(proj.at[:, mz], proj.at[:, mz], z_send.at[k], z_recv.at[k], zat(dz))
    lam_copies = [send(lam.at[mz], lam.at[mz], lam_send.at[k], lam_recv.at[k], zat(dz)) for k, dz in enumerate(SLOTS)]

    for slot in (1, 3):
        for half in range(2):
            p1[half, slot].wait_recv()
            forward(half, slot)
    for half in range(2):
        p1[half, 2].wait_recv()
        forward(half, 2)

    z_copies[1].wait_recv()
    below = (mz + 3) % NZ
    zf = [send(proj.at[pl.ds(0, 32), below], proj.at[pl.ds(0, 32), below], zf_send.at[0], zf_recv.at[0], zat(1))]
    z_copies[3].wait_recv()
    above = (mz + 1) % NZ
    zf.append(send(proj.at[pl.ds(32, 32), above], proj.at[pl.ds(32, 32), above], zf_send.at[1], zf_recv.at[1], zat(3)))

    loads[7].wait()
    lam_g[...] = jnp.zeros_like(lam_g)
    cross[...] = jnp.zeros_like(cross)

    def proj_g(half, slot):
        for e in range(8):
            if slot == 0 and e == 0:
                continue
            (p1e[half, slot] if e == 0 else p2[half, slot, e]).wait_recv()
        g = half * 4 + slot

        def step(n, carry):
            cols = pl.ds(pl.multiple_of(n * TILE, TILE), TILE)
            value = jnp.dot(
                rows[pl.ds(g * 8, 8)].reshape(512, BLK), bg[:, cols], preferred_element_type=jnp.float32
            )
            lam_g[:, cols] += jnp.sum((value * value).reshape(64, 8, TILE), axis=0)
            graw[g, :, :, cols] = value.astype(jnp.bfloat16).reshape(4, 128, TILE)
            return carry

        lax.fori_loop(0, 4, step, 0)

    def cross_step(step, carry):
        g, p, q = step // 8, (step // 2) % 4, step % 2
        prows = pl.ds(pl.multiple_of(p * TILE, TILE), TILE)
        cols = pl.ds(pl.multiple_of(q * 512, 512), 512)
        left = proj[pl.ds(g * 8, 8), :, :, prows].reshape(512, TILE)
        cross[prows, cols] += lax.dot_general(
            left, graw[g, :, :, cols].reshape(512, 512), (((0,), (0,)), ((), ())), preferred_element_type=jnp.float32
        )
        return carry

    for slot in (0, 1, 3):
        for half in range(2):
            proj_g(half, slot)
    for copy in zf:
        copy.wait_recv()
    for copy in lam_copies:
        copy.wait_recv()
    for g0, g1 in ((0, 2), (3, 6), (7, 8)):
        lax.fori_loop(g0 * 8, g1 * 8, cross_step, 0)
    proj_g(0, 2)
    lax.fori_loop(2 * 8, 3 * 8, cross_step, 0)
    proj_g(1, 2)
    lax.fori_loop(6 * 8, 7 * 8, cross_step, 0)

    total = cnt_ref[0]
    for s in range(1, N_DP):
        total += cnt_ref[s]
    row_total = total.astype(jnp.float32)

    sum_a = jnp.sum(lam[0] + lam[1] + lam[2] + lam[3], axis=0, keepdims=True)
    lam_a[...] = jnp.broadcast_to(sum_a, (8, BLK)) / row_total
    lam_g[...] = jnp.broadcast_to(jnp.sum(lam_g[...], axis=0, keepdims=True), (8, BLK)) / row_total

    def right_step(p, carry):
        prows = pl.ds(pl.multiple_of(p * TILE, TILE), TILE)
        col_a = jnp.transpose(lam_a[:, prows], (1, 0))[:, 0:1]
        scaled = (cross[prows, :] / row_total) / (col_a * lam_g[0:1, :] + damping)
        scaled = scaled.astype(jnp.bfloat16)
        for n in range(4):
            baraw[4 + p, :, n * TILE : (n + 1) * TILE] = lax.dot_general(
                scaled, bg[n * TILE : (n + 1) * TILE, :], (((1,), (1,)), ((), ())), preferred_element_type=jnp.float32
            ).astype(jnp.bfloat16)
        return carry

    lax.fori_loop(0, 4, right_step, 0)

    for copy in act_copies:
        copy.wait_send()

    def out_step(step, carry):
        t, cols = step // 4, pl.ds(pl.multiple_of((step % 4) * TILE, TILE), TILE)
        value = jnp.dot(
            basis[t], baraw[pl.ds(4, 4), :, cols].reshape(BLK, TILE), preferred_element_type=jnp.float32
        )
        sa[pl.ds(t * 8, 8), :, cols] = value.astype(jnp.bfloat16).reshape(8, 32, TILE)
        return carry

    lax.fori_loop(0, 16, out_step, 0)
    out_copies = []
    for disp in SPREAD:
        i, target = index_of(*disp), at(*disp)
        out_copies.append(send(sa.at[target], back.at[me], out_send.at[i], out_recv.at[i], (target, mz)))
    back[me] = sa[me]
    for copy in out_copies:
        copy.wait_recv()
    stores = []
    for part in range(4):
        for u in range(part * 8, part * 8 + 8):
            ra[u] = back[own_ref[u]]
        stores.append(
            pltpu.make_async_copy(ra.at[pl.ds(part * 8, 8)], out_hbm.at[pl.ds(part * 8, 8)], store_sem.at[part])
        )
        stores[-1].start()
    for copy in stores:
        copy.wait()
    for copy in out_copies + ba_copies + lam_copies + zf + list(z_copies.values()):
        copy.wait_send()
    for copies in (p1, p1e, p2):
        for copy in copies.values():
            copy.wait_send()


def local(acts, grads_out, counts, owners, bases_a, bases_g):
    slot_ids = jnp.arange(N_DP, dtype=jnp.int32)
    inverse = jnp.sum((owners[None, :] == slot_ids[:, None]).astype(jnp.int32) * slot_ids[None, :], axis=1)
    smem = pl.BlockSpec(memory_space=pltpu.SMEM)
    hbm = pl.BlockSpec(memory_space=pl.ANY)
    bf16, f32 = jnp.bfloat16, jnp.float32
    dma = pltpu.SemaphoreType.DMA
    result = pl.pallas_call(
        kernel,
        out_shape=jax.ShapeDtypeStruct((N_DP, 32, BLK), bf16),
        in_specs=[smem, smem, smem, hbm, hbm, hbm, hbm],
        out_specs=hbm,
        scratch_shapes=[
            pltpu.VMEM((8, 4, 128, BLK), bf16),
            pltpu.VMEM((8, 2, SUB, BLK), bf16),
            pltpu.VMEM((8, 256, BLK), bf16),
            pltpu.VMEM((BLK, BLK), bf16),
            pltpu.VMEM((2, 3, 8, HALF, BLK), bf16),
            pltpu.VMEM((2, 4, 7, HALF, BLK), bf16),
            pltpu.VMEM((64, HALF, BLK), bf16),
            pltpu.VMEM((N_DP, 32, BLK), bf16),
            pltpu.VMEM((N_DP, 32, BLK), bf16),
            pltpu.VMEM((64, NZ, SUB, BLK), bf16),
            pltpu.VMEM((NZ, 256, BLK), bf16),
            pltpu.VMEM((NZ, 8, BLK), f32),
            pltpu.VMEM((8, BLK), f32),
        pltpu.VMEM((8, BLK), f32),
            pltpu.VMEM((BLK, BLK), f32),
            pltpu.VMEM((N_DP, 32, BLK), bf16),
            pltpu.VMEM((HALF, BLK), bf16),
            dma((8,)),
            dma((N_DP,)), dma((N_DP,)),
            dma((3,)), dma((3,)),
            dma((3,)), dma((3,)),
            dma((2, 4)), dma((2, 4)),
            dma((2, 4)), dma((2, 4)),
            dma((2, 4, 8)), dma((2, 4, 8)),
            dma((2,)), dma((2,)),
            dma((2,)), dma((2,)),
            dma((N_DP,)), dma((N_DP,)),
            dma((4,)),
        ],
        compiler_params=pltpu.CompilerParams(
            collective_id=0, has_side_effects=True, vmem_limit_bytes=63 * 1024 * 1024
        ),
        name="kfac",
    )(inverse, owners, counts, acts, grads_out, bases_a, bases_g.reshape(BLK, BLK))
    return result.reshape(8, 4, 32, BLK)


def solution(mesh):
    placed = (
        P(None, "dp", None),
        P(None, "dp", "mp"),
        P(),
        P(),
        P(None, "mp", None),
        P("mp", "dp", None, None),
    )
    return jax.shard_map(
        local, mesh=mesh, in_specs=placed, out_specs=P(None, "mp", "dp", None), check_vma=False
    )
```

```python
import functools

import jax
import jax.numpy as jnp
from jax import lax
from jax.experimental import pallas as pl
from jax.experimental.pallas import tpu as pltpu
from jax.sharding import PartitionSpec as P

MESH = pl.DeviceIdType.MESH
damping = 0.0001
BLK = 1024
TILE = 256
HCOL = 512
NY, NX, NC, NZ = 4, 4, 2, 4
N_DP = NY * NX * NC
HALF = 64
SUB = HALF // NZ

PAIRS = [(2, 2), (1, 3), (3, 1), (2, 0), (0, 2), (1, 1), (3, 3), (2, 1), (2, 3), (1, 2), (3, 2), (0, 1), (1, 0), (0, 3), (3, 0)]
SPREAD = [(dy, dx, dc) for dc in range(NC) for dy, dx in PAIRS] + [(0, 0, 1)]
SLOTS = (1, 3, 2)


def kernel(
    inv_ref, own_ref, cnt_ref, acts_hbm, grads_hbm, ba_hbm, bg_hbm, out_hbm,
    graw, araw, baraw, bg, first, mid, rows, sa, ra, proj, basis, lam, lam_g, cross, back, mask,
    load_sem, act_send, act_recv, ba_send, ba_recv, lam_send, lam_recv,
    p1_send, p1_recv, p1e_send, p1e_recv, p2_send, p2_recv, z_send, z_recv, zf_send, zf_recv, out_send, out_recv, store_sem,
):
    me, mz = lax.axis_index("dp"), lax.axis_index("mp")
    my, mx, mc = me // 8, (me // 2) % 4, me % 2

    def at(dy, dx, dc):
        return ((my + dy) % NY) * 8 + ((mx + dx) % NX) * 2 + (mc + dc) % NC

    def zat(dz):
        return (me, (mz + dz) % NZ)

    def send(src, dst, ssem, rsem, target):
        copy = pltpu.make_async_remote_copy(
            src_ref=src, dst_ref=dst, send_sem=ssem, recv_sem=rsem, device_id=target, device_id_type=MESH
        )
        copy.start()
        return copy

    loads = [
        pltpu.make_async_copy(acts_hbm.at[:, pl.ds(mz * SUB, SUB)], araw.at[:, 0], load_sem.at[0]),
        pltpu.make_async_copy(acts_hbm.at[:, pl.ds(HALF + mz * SUB, SUB)], araw.at[:, 1], load_sem.at[1]),
        pltpu.make_async_copy(ba_hbm, baraw, load_sem.at[2]),
    ]
    for j in range(8):
        loads.append(
            pltpu.make_async_copy(grads_hbm.at[:, :, pl.ds(j * HCOL, HCOL)], graw.at[j], load_sem.at[3 + j])
        )
    loads.append(pltpu.make_async_copy(bg_hbm, bg, load_sem.at[11]))
    for copy in loads:
        copy.start()

    barrier = pltpu.get_barrier_semaphore()
    peers = [(at(*d), mz) for d in SPREAD] + [zat(dz) for dz in (1, 2, 3)]
    for peer in peers:
        pl.semaphore_signal(barrier, inc=1, device_id=peer, device_id_type=MESH)

    live = cnt_ref[me] - HALF
    row_ids = lax.broadcasted_iota(jnp.int32, (HALF, BLK), 0)
    mask[...] = jnp.where(row_ids < live, 1.0, 0.0).astype(jnp.bfloat16)

    loads[0].wait()
    loads[1].wait()
    pl.semaphore_wait(barrier, len(peers))

    sub_mask = mask[pl.ds(pl.multiple_of(mz * SUB, SUB), SUB), :]

    def pack_acts(dst, index, disp):
        layer = inv_ref[at(*disp)] // 4
        dst[index, pl.ds(0, SUB), :] = araw[layer, 0]
        dst[index, pl.ds(SUB, SUB), :] = araw[layer, 1] * sub_mask

    def index_of(dy, dx, dc):
        return (dy * 4 + dx) * 2 + dc

    act_copies = []
    for disp in SPREAD:
        i = index_of(*disp)
        pack_acts(sa, i, disp)
        act_copies.append(send(sa.at[i], ra.at[i], act_send.at[i], act_recv.at[i], (at(*disp), mz)))
    pack_acts(ra, 0, (0, 0, 0))

    loads[2].wait()
    basis[mz] = baraw[inv_ref[me] // 4]
    ba_copies = [
        send(basis.at[mz], basis.at[mz], ba_send.at[k], ba_recv.at[k], zat(dz)) for k, dz in enumerate(SLOTS)
    ]

    for j in range(8):
        loads[3 + j].wait()

    def disp_of(half, slot, e):
        other, dc = e // 2, e % 2
        return (other, slot, dc) if half == 0 else (slot, other, dc)

    def hop(half, slot):
        return (at(0, slot, 0) if half == 0 else at(slot, 0, 0), mz)

    def pack(dst, half, disp):
        unit = inv_ref[at(*disp)]
        layer, column = unit // 4, unit % 4
        for c in range(2):
            cols = pl.ds(c * HCOL, HCOL)
            block = graw[column * 2 + c, layer, pl.ds(half * HALF, HALF), :]
            dst[:, cols] = block if half == 0 else block * mask[:, cols]

    p1, p1e, p2 = {}, {}, {}
    def forward(half, slot):
        for e in (4, 5, 2, 6, 3, 7, 1):
            disp = (e // 2, 0, e % 2) if half == 0 else (0, e // 2, e % 2)
            p2[half, slot, e] = send(
                mid.at[half, slot, e - 1], rows.at[(half * 4 + slot) * 8 + e],
                p2_send.at[half, slot, e], p2_recv.at[half, slot, e], (at(*disp), mz),
            )

    def start_slot(slot):
        for half in range(2):
            for e in range(8):
                pack(first.at[half, slot - 1, e], half, disp_of(half, slot, e))
            p1[half, slot] = send(
                first.at[half, slot - 1, pl.ds(1, 7)], mid.at[half, slot],
                p1_send.at[half, slot], p1_recv.at[half, slot], hop(half, slot),
            )
            p1e[half, slot] = send(
                first.at[half, slot - 1, 0], rows.at[(half * 4 + slot) * 8],
                p1e_send.at[half, slot], p1e_recv.at[half, slot], hop(half, slot),
            )

    for half in range(2):
        for e in range(1, 8):
            pack(mid.at[half, 0, e - 1], half, disp_of(half, 0, e))
        pack(rows.at[half * 32], half, disp_of(half, 0, 0))
        forward(half, 0)
    start_slot(1)
    start_slot(3)
    start_slot(2)

    loads[11].wait()
    for k in range(4):
        baraw[k] = jnp.transpose(bg[:, k * TILE : (k + 1) * TILE], (1, 0))

    for copy in act_copies:
        copy.wait_recv()
    for copy in ba_copies:
        copy.wait_recv()
    lam[mz] = jnp.zeros((8, BLK), jnp.float32)
    lam_g[...] = jnp.zeros_like(lam_g)
    cross[...] = jnp.zeros_like(cross)

    def proj_a_step(step, carry):
        block = ra[pl.ds(step * 16, 16)].reshape(512, BLK)
        value = jnp.dot(block, basis[...].reshape(BLK, BLK), preferred_element_type=jnp.float32)
        lam[mz] += jnp.sum((value * value).reshape(64, 8, BLK), axis=0)
        value = value.astype(jnp.bfloat16)
        for y in range(2):
            dy = step * 2 + y
            for dx in range(4):
                for dc in range(2):
                    r = (y * 8 + dx * 2 + dc) * 32
                    proj[dx * 8 + dy * 2 + dc, mz] = value[r : r + SUB]
                    proj[(4 + dy) * 8 + dx * 2 + dc, mz] = value[r + SUB : r + 2 * SUB]
        return carry

    lax.fori_loop(0, 2, proj_a_step, 0)

    z_copies = {}
    for k, dz in enumerate((1, 3)):
        z_copies[dz] = send(proj.at[:, mz], proj.at[:, mz], z_send.at[k], z_recv.at[k], zat(dz))
    lam_copies = [send(lam.at[mz], lam.at[mz], lam_send.at[k], lam_recv.at[k], zat(dz)) for k, dz in enumerate(SLOTS)]

    for slot in (1, 3):
        for half in range(2):
            p1[half, slot].wait_recv()
            forward(half, slot)
    for half in range(2):
        p1[half, 2].wait_recv()
        forward(half, 2)

    z_copies[1].wait_recv()
    below = (mz + 3) % NZ
    zf = [send(proj.at[pl.ds(0, 32), below], proj.at[pl.ds(0, 32), below], zf_send.at[0], zf_recv.at[0], zat(1))]
    z_copies[3].wait_recv()
    above = (mz + 1) % NZ
    zf.append(send(proj.at[pl.ds(32, 32), above], proj.at[pl.ds(32, 32), above], zf_send.at[1], zf_recv.at[1], zat(3)))

    def proj_g(half, slot):
        for e in range(8):
            if slot == 0 and e == 0:
                continue
            (p1e[half, slot] if e == 0 else p2[half, slot, e]).wait_recv()
        g = half * 4 + slot
        value = lax.dot_general(
            baraw[pl.ds(0, 4)].reshape(BLK, BLK), rows[pl.ds(g * 8, 8)].reshape(512, BLK),
            (((1,), (1,)), ((), ())), preferred_element_type=jnp.float32,
        )
        square = value * value
        lam_g[...] += square[:, 0:128] + square[:, 128:256] + square[:, 256:384] + square[:, 384:512]
        graw[g] = value.astype(jnp.bfloat16).reshape(8, 128, HCOL)

    def cross_part(g, part):
        return jnp.dot(
            graw[g, pl.ds(part * 4, 4)].reshape(512, HCOL), proj[pl.ds(g * 8, 8)].reshape(512, BLK),
            preferred_element_type=jnp.float32,
        )

    def add_cross(half, slot):
        for part in range(2):
            cross[pl.ds(part * 512, 512), :] += cross_part(half * 4 + slot, part)

    for slot in (0, 1, 3):
        for half in range(2):
            proj_g(half, slot)
    for copy in zf + lam_copies:
        copy.wait_recv()
    for slot in (0, 1, 3):
        for half in range(2):
            add_cross(half, slot)
    proj_g(0, 2)
    add_cross(0, 2)
    proj_g(1, 2)

    total = cnt_ref[0]
    for s in range(1, N_DP):
        total += cnt_ref[s]
    row_total = total.astype(jnp.float32)
    row_a = jnp.sum(lam[0] + lam[1] + lam[2] + lam[3], axis=0, keepdims=True) / row_total
    col_g = jnp.sum(lam_g[...], axis=1, keepdims=True) / row_total
    for part in range(2):
        prows = slice(part * 512, part * 512 + 512)
        value = (cross[prows, :] + cross_part(6, part)) / row_total
        scaled = value / (col_g[prows] * row_a + damping)
        baraw[4 + part * 2 : 6 + part * 2] = scaled.astype(jnp.bfloat16).reshape(2, 256, BLK)

    for copies in (act_copies, p1.values(), p1e.values()):
        for copy in copies:
            copy.wait_send()

    out_copies = []
    for part in range(2):
        prows, cols = pl.ds(part * 512, 512), pl.ds(part * HCOL, HCOL)
        first[0, part] = jnp.dot(
            bg[prows, :], baraw[pl.ds(4, 4)].reshape(BLK, BLK), preferred_element_type=jnp.float32
        ).astype(jnp.bfloat16).reshape(8, HALF, BLK)
        sa[:, :, cols] = lax.dot_general(
            basis[...].reshape(BLK, BLK), first[0, part].reshape(512, BLK), (((1,), (1,)), ((), ())),
            preferred_element_type=jnp.float32,
        ).astype(jnp.bfloat16).reshape(N_DP, 32, HCOL)
        for disp in SPREAD:
            i, target = index_of(*disp), at(*disp)
            out_copies.append(
                send(
                    sa.at[target, :, cols], back.at[me, :, cols],
                    out_send.at[part, i], out_recv.at[part, i], (target, mz),
                )
            )
    back[me] = sa[me]
    for copy in out_copies:
        copy.wait_recv()
    stores = []
    for part in range(4):
        for u in range(part * 8, part * 8 + 8):
            ra[u] = back[own_ref[u]]
        stores.append(
            pltpu.make_async_copy(ra.at[pl.ds(part * 8, 8)], out_hbm.at[pl.ds(part * 8, 8)], store_sem.at[part])
        )
        stores[-1].start()
    for copy in stores:
        copy.wait()
    for copy in out_copies + ba_copies + lam_copies + zf + list(z_copies.values()) + list(p2.values()):
        copy.wait_send()


def local(acts, grads_out, counts, owners, bases_a, bases_g):
    slot_ids = jnp.arange(N_DP, dtype=jnp.int32)
    inverse = jnp.sum((owners[None, :] == slot_ids[:, None]).astype(jnp.int32) * slot_ids[None, :], axis=1)
    smem = pl.BlockSpec(memory_space=pltpu.SMEM)
    hbm = pl.BlockSpec(memory_space=pl.ANY)
    bf16, f32 = jnp.bfloat16, jnp.float32
    dma = pltpu.SemaphoreType.DMA
    result = pl.pallas_call(
        kernel,
        out_shape=jax.ShapeDtypeStruct((N_DP, 32, BLK), bf16),
        in_specs=[smem, smem, smem, hbm, hbm, hbm, hbm],
        out_specs=hbm,
        scratch_shapes=[
            pltpu.VMEM((8, 8, 128, HCOL), bf16),
            pltpu.VMEM((8, 2, SUB, BLK), bf16),
            pltpu.VMEM((8, 256, BLK), bf16),
            pltpu.VMEM((BLK, BLK), bf16),
            pltpu.VMEM((2, 3, 8, HALF, BLK), bf16),
            pltpu.VMEM((2, 4, 7, HALF, BLK), bf16),
            pltpu.VMEM((64, HALF, BLK), bf16),
            pltpu.VMEM((N_DP, 32, BLK), bf16),
            pltpu.VMEM((N_DP, 32, BLK), bf16),
            pltpu.VMEM((64, NZ, SUB, BLK), bf16),
            pltpu.VMEM((NZ, 256, BLK), bf16),
            pltpu.VMEM((NZ, 8, BLK), f32),
            pltpu.VMEM((BLK, 128), f32),
            pltpu.VMEM((BLK, BLK), f32),
            pltpu.VMEM((N_DP, 32, BLK), bf16),
            pltpu.VMEM((HALF, BLK), bf16),
            dma((12,)),
            dma((N_DP,)), dma((N_DP,)),
            dma((3,)), dma((3,)),
            dma((3,)), dma((3,)),
            dma((2, 4)), dma((2, 4)),
            dma((2, 4)), dma((2, 4)),
            dma((2, 4, 8)), dma((2, 4, 8)),
            dma((2,)), dma((2,)),
            dma((2,)), dma((2,)),
            dma((2, N_DP)), dma((2, N_DP)),
            dma((4,)),
        ],
        compiler_params=pltpu.CompilerParams(
            collective_id=0, has_side_effects=True, vmem_limit_bytes=63 * 1024 * 1024
        ),
        name="kfac",
    )(inverse, owners, counts, acts, grads_out, bases_a, bases_g.reshape(BLK, BLK))
    return result.reshape(8, 4, 32, BLK)


def solution(mesh):
    placed = (
        P(None, "dp", None),
        P(None, "dp", "mp"),
        P(),
        P(),
        P(None, "mp", None),
        P("mp", "dp", None, None),
    )
    return jax.shard_map(
        local, mesh=mesh, in_specs=placed, out_specs=P(None, "mp", "dp", None), check_vma=False
    )
```

```python
import functools

import jax
import jax.numpy as jnp
from jax import lax
from jax.experimental import pallas as pl
from jax.experimental.pallas import tpu as pltpu
from jax.sharding import PartitionSpec as P

MESH = pl.DeviceIdType.MESH
damping = 0.0001
BLK = 1024
TILE = 256
HCOL = 512
NY, NX, NC, NZ = 4, 4, 2, 4
N_DP = NY * NX * NC
HALF = 64
SUB = HALF // NZ

PAIRS = [(2, 2), (1, 3), (3, 1), (2, 0), (0, 2), (1, 1), (3, 3), (2, 1), (2, 3), (1, 2), (3, 2), (0, 1), (1, 0), (0, 3), (3, 0)]
SPREAD = [(dy, dx, dc) for dc in range(NC) for dy, dx in PAIRS] + [(0, 0, 1)]
SLOTS = (1, 3, 2)
SECOND = [(0, 0), (0, 1), (2, 0), (2, 1), (1, 0), (3, 0), (1, 1), (3, 1)]
COLS = 256


def kernel(
    own_ref, cnt_ref, acts_hbm, grads_hbm, ba_hbm, bg_hbm, out_hbm,
    graw, araw, baraw, bg, first, mid, rows, sa, ra, proj, basis, lam, lam_g, cross, mask, inv_ref,
    load_sem, act_send, act_recv, ba_send, ba_recv, lam_send, lam_recv,
    p1_send, p1_recv, p1e_send, p1e_recv, p2_send, p2_recv, z_send, z_recv, zf_send, zf_recv, out_send, out_recv, store_sem,
):
    me, mz = lax.axis_index("dp"), lax.axis_index("mp")
    my, mx, mc = me // 8, (me // 2) % 4, me % 2

    def at(dy, dx, dc):
        return ((my + dy) % NY) * 8 + ((mx + dx) % NX) * 2 + (mc + dc) % NC

    def zat(dz):
        return (me, (mz + dz) % NZ)

    def send(src, dst, ssem, rsem, target):
        copy = pltpu.make_async_remote_copy(
            src_ref=src, dst_ref=dst, send_sem=ssem, recv_sem=rsem, device_id=target, device_id_type=MESH
        )
        copy.start()
        return copy

    loads = [
        pltpu.make_async_copy(acts_hbm.at[:, pl.ds(mz * SUB, SUB)], araw.at[:, 0], load_sem.at[0]),
        pltpu.make_async_copy(acts_hbm.at[:, pl.ds(HALF + mz * SUB, SUB)], araw.at[:, 1], load_sem.at[1]),
    ]
    for j in range(8):
        loads.append(
            pltpu.make_async_copy(grads_hbm.at[:, :, pl.ds(j * HCOL, HCOL)], graw.at[j], load_sem.at[2 + j])
        )
    loads.append(pltpu.make_async_copy(ba_hbm, baraw, load_sem.at[10]))
    loads.append(pltpu.make_async_copy(bg_hbm, bg, load_sem.at[11]))
    for copy in loads:
        copy.start()

    barrier = pltpu.get_barrier_semaphore()
    peers = [(at(*d), mz) for d in SPREAD] + [zat(dz) for dz in (1, 2, 3)]
    for peer in peers:
        pl.semaphore_signal(barrier, inc=1, device_id=peer, device_id_type=MESH)

    def invert(d, carry):
        unit = jnp.int32(0)
        for u in range(1, N_DP):
            unit = jnp.where(own_ref[u] == d, u, unit)
        inv_ref[d] = unit
        return carry

    lax.fori_loop(0, N_DP, invert, 0)

    live = cnt_ref[me] - HALF
    row_ids = lax.broadcasted_iota(jnp.int32, (HALF, BLK), 0)
    mask[...] = jnp.where(row_ids < live, 1.0, 0.0).astype(jnp.bfloat16)

    sub_mask = mask[pl.ds(pl.multiple_of(mz * SUB, SUB), SUB), :]

    def pack_acts(dst, index, disp):
        layer = inv_ref[at(*disp)] // 4
        dst[index, pl.ds(0, SUB), :] = araw[layer, 0]
        dst[index, pl.ds(SUB, SUB), :] = araw[layer, 1] * sub_mask

    def index_of(dy, dx, dc):
        return (dy * 4 + dx) * 2 + dc

    loads[0].wait()
    loads[1].wait()
    for disp in SPREAD:
        pack_acts(sa, index_of(*disp), disp)
    pack_acts(ra, 0, (0, 0, 0))

    def disp_of(half, slot, e):
        other, dc = SECOND[e]
        return (other, slot, dc) if half == 0 else (slot, other, dc)

    def hop(half, slot):
        return (at(0, slot, 0) if half == 0 else at(slot, 0, 0), mz)

    def pack(dst, half, disp):
        unit = inv_ref[at(*disp)]
        layer, column = unit // 4, unit % 4
        for c in range(2):
            cols = pl.ds(c * HCOL, HCOL)
            block = graw[column * 2 + c, layer, pl.ds(half * HALF, HALF), :]
            dst[:, cols] = block if half == 0 else block * mask[:, cols]

    p1, p1e, p2 = {}, {}, {}

    def forward(half, slot):
        for e in range(2, 9):
            e = 1 if e == 8 else e
            other, dc = SECOND[e]
            p2[half, slot, e] = send(
                mid.at[half, slot, e - 1], rows.at[(half * 4 + slot) * 8 + e],
                p2_send.at[half, slot, e], p2_recv.at[half, slot, e],
                (at(other, 0, dc) if half == 0 else at(0, other, dc), mz),
            )

    def pack_slot(slot):
        for half in range(2):
            for e in range(8):
                pack(first.at[half, slot - 1, e], half, disp_of(half, slot, e))

    def start_slot(slot):
        for half in range(2):
            p1[half, slot] = send(
                first.at[half, slot - 1, pl.ds(1, 7)], mid.at[half, slot],
                p1_send.at[half, slot], p1_recv.at[half, slot], hop(half, slot),
            )
            p1e[half, slot] = send(
                first.at[half, slot - 1, 0], rows.at[(half * 4 + slot) * 8],
                p1e_send.at[half, slot], p1e_recv.at[half, slot], hop(half, slot),
            )

    for j in range(8):
        loads[2 + j].wait()
    for half in range(2):
        for e in range(1, 8):
            pack(mid.at[half, 0, e - 1], half, disp_of(half, 0, e))
        pack(rows.at[half * 32], half, disp_of(half, 0, 0))
    loads[10].wait()
    basis[mz] = baraw[inv_ref[me] // 4]

    pl.semaphore_wait(barrier, len(peers))
    act_copies = []
    for disp in SPREAD:
        i = index_of(*disp)
        act_copies.append(send(sa.at[i], ra.at[i], act_send.at[i], act_recv.at[i], (at(*disp), mz)))
    ba_copies = [
        send(basis.at[mz], basis.at[mz], ba_send.at[k], ba_recv.at[k], zat(dz)) for k, dz in enumerate(SLOTS)
    ]
    forward(0, 0)
    forward(1, 0)
    for slot in SLOTS:
        pack_slot(slot)
        start_slot(slot)

    loads[11].wait()
    for k in range(4):
        baraw[k] = jnp.transpose(bg[:, k * TILE : (k + 1) * TILE], (1, 0))

    for copy in act_copies:
        copy.wait_recv()
    for copy in ba_copies:
        copy.wait_recv()
    lam[mz] = jnp.zeros((8, BLK), jnp.float32)
    lam_g[...] = jnp.zeros_like(lam_g)
    cross[...] = jnp.zeros_like(cross)

    def proj_a_step(step, carry):
        block = ra[pl.ds(step * 16, 16)].reshape(512, BLK)
        value = jnp.dot(block, basis[...].reshape(BLK, BLK), preferred_element_type=jnp.float32)
        lam[mz] += jnp.sum((value * value).reshape(64, 8, BLK), axis=0)
        value = value.astype(jnp.bfloat16)
        for y in range(2):
            dy = step * 2 + y
            for dx in range(4):
                for dc in range(2):
                    r = (y * 8 + dx * 2 + dc) * 32
                    e = 2 * step + dc if y == 0 else 4 + step + 2 * dc
                    proj[dx * 8 + e, mz] = value[r : r + SUB]
                    proj[(4 + dy) * 8 + SECOND.index((dx, dc)), mz] = value[r + SUB : r + 2 * SUB]
        return carry

    lax.fori_loop(0, 2, proj_a_step, 0)

    z_copies = {}
    for k, dz in enumerate((1, 3)):
        z_copies[dz] = send(proj.at[:, mz], proj.at[:, mz], z_send.at[k], z_recv.at[k], zat(dz))
    lam_copies = [send(lam.at[mz], lam.at[mz], lam_send.at[k], lam_recv.at[k], zat(dz)) for k, dz in enumerate(SLOTS)]

    for slot in (1, 3):
        for half in range(2):
            p1[half, slot].wait_recv()
            forward(half, slot)
    for half in range(2):
        p1[half, 2].wait_recv()
        forward(half, 2)

    z_copies[1].wait_recv()
    below = (mz + 3) % NZ
    zf = [send(proj.at[pl.ds(0, 32), below], proj.at[pl.ds(0, 32), below], zf_send.at[0], zf_recv.at[0], zat(1))]
    z_copies[3].wait_recv()
    above = (mz + 1) % NZ
    zf.append(send(proj.at[pl.ds(32, 32), above], proj.at[pl.ds(32, 32), above], zf_send.at[1], zf_recv.at[1], zat(3)))

    def arrived(half, slot, blocks):
        for e in blocks:
            if slot == 0 and e == 0:
                continue
            (p1e[half, slot] if e == 0 else p2[half, slot, e]).wait_recv()

    def project(block):
        value = lax.dot_general(
            baraw[pl.ds(0, 4)].reshape(BLK, BLK), block, (((1,), (1,)), ((), ())), preferred_element_type=jnp.float32
        )
        square = value * value
        part = square[:, 0:128]
        for k in range(1, block.shape[0] // 128):
            part += square[:, k * 128 : (k + 1) * 128]
        lam_g[...] += part
        return value.astype(jnp.bfloat16)

    def proj_g(slot, count):
        def step(half, carry):
            g = half * 4 + slot
            value = project(rows[pl.ds(g * 8, count)].reshape(count * HALF, BLK))
            graw[g, :, :, pl.ds(0, count * HALF)] = value.reshape(8, 128, count * HALF)
            return carry

        for half in range(2):
            arrived(half, slot, range(count))
        lax.fori_loop(0, 2, step, 0)

    def add_cross(slot, count):
        def step(i, carry):
            half, part = i // 2, i % 2
            g = half * 4 + slot
            right = proj[pl.ds(g * 8, count)].reshape(count * HALF, BLK)
            left = graw[g, pl.ds(part * 4, 4), :, pl.ds(0, count * HALF)].reshape(512, count * HALF)
            prows = pl.ds(pl.multiple_of(part * 512, 512), 512)
            cross[prows, :] += jnp.dot(left, right, preferred_element_type=jnp.float32)
            return carry

        lax.fori_loop(0, 4, step, 0)

    for slot in (0, 1, 3):
        proj_g(slot, 8)
    for copy in zf + lam_copies:
        copy.wait_recv()
    for slot in (0, 1, 3):
        add_cross(slot, 8)
    proj_g(2, 6)
    add_cross(2, 6)
    for half in range(2):
        arrived(half, 2, (6, 7))
    last_g = project(
        jnp.concatenate([rows[pl.ds((half * 4 + 2) * 8 + 6, 2)].reshape(128, BLK) for half in range(2)], axis=0)
    )
    last_a = jnp.concatenate([proj[pl.ds((half * 4 + 2) * 8 + 6, 2)].reshape(128, BLK) for half in range(2)], axis=0)

    total = cnt_ref[0]
    for s in range(1, N_DP):
        total += cnt_ref[s]
    row_total = total.astype(jnp.float32)
    row_a = jnp.sum(lam[0] + lam[1] + lam[2] + lam[3], axis=0, keepdims=True) / row_total
    col_g = jnp.sum(lam_g[...], axis=1, keepdims=True) / row_total
    for part in range(2):
        prows = slice(part * 512, part * 512 + 512)
        value = cross[prows, :] + jnp.dot(last_g[prows], last_a, preferred_element_type=jnp.float32)
        scaled = (value / row_total) / (col_g[prows] * row_a + damping)
        baraw[4 + part * 2 : 6 + part * 2] = scaled.astype(jnp.bfloat16).reshape(2, 256, BLK)

    for copies in (act_copies, p1.values(), p1e.values()):
        for copy in copies:
            copy.wait_send()

    out_copies = []
    for part in range(4):
        prows, cols = pl.ds(part * COLS, COLS), pl.ds(part * COLS, COLS)
        right = jnp.dot(
            bg[prows, :], baraw[pl.ds(4, 4)].reshape(BLK, BLK), preferred_element_type=jnp.float32
        ).astype(jnp.bfloat16)
        sa[:, :, cols] = lax.dot_general(
            basis[...].reshape(BLK, BLK), right, (((1,), (1,)), ((), ())), preferred_element_type=jnp.float32
        ).astype(jnp.bfloat16).reshape(N_DP, 32, COLS)
        for disp in SPREAD:
            i, target = index_of(*disp), at(*disp)
            out_copies.append(
                send(
                    sa.at[target, :, cols], out_hbm.at[me, :, cols],
                    out_send.at[part, i], out_recv.at[part, i], (target, mz),
                )
            )
    own = pltpu.make_async_copy(sa.at[me], out_hbm.at[me], store_sem)
    own.start()
    for copy in out_copies:
        copy.wait_recv()
    own.wait()
    for copy in out_copies + ba_copies + lam_copies + zf + list(z_copies.values()) + list(p2.values()):
        copy.wait_send()


def order_kernel(own_ref, pieces_hbm, out_hbm, sem):
    copies = [
        pltpu.make_async_copy(pieces_hbm.at[own_ref[u]], out_hbm.at[u // 4, u % 4], sem.at[u]) for u in range(N_DP)
    ]
    for copy in copies:
        copy.start()
    for copy in copies:
        copy.wait()


def local(acts, grads_out, counts, owners, bases_a, bases_g):
    smem = pl.BlockSpec(memory_space=pltpu.SMEM)
    hbm = pl.BlockSpec(memory_space=pl.ANY)
    bf16, f32 = jnp.bfloat16, jnp.float32
    dma = pltpu.SemaphoreType.DMA
    pieces = pl.pallas_call(
        kernel,
        out_shape=jax.ShapeDtypeStruct((N_DP, 32, BLK), bf16),
        in_specs=[smem, smem, hbm, hbm, hbm, hbm],
        out_specs=hbm,
        scratch_shapes=[
            pltpu.VMEM((8, 8, 128, HCOL), bf16),
            pltpu.VMEM((8, 2, SUB, BLK), bf16),
            pltpu.VMEM((8, 256, BLK), bf16),
            pltpu.VMEM((BLK, BLK), bf16),
            pltpu.VMEM((2, 3, 8, HALF, BLK), bf16),
            pltpu.VMEM((2, 4, 7, HALF, BLK), bf16),
            pltpu.VMEM((64, HALF, BLK), bf16),
            pltpu.VMEM((N_DP, 32, BLK), bf16),
            pltpu.VMEM((N_DP, 32, BLK), bf16),
            pltpu.VMEM((64, NZ, SUB, BLK), bf16),
            pltpu.VMEM((NZ, 256, BLK), bf16),
            pltpu.VMEM((NZ, 8, BLK), f32),
            pltpu.VMEM((BLK, 128), f32),
            pltpu.VMEM((BLK, BLK), f32),
            pltpu.VMEM((HALF, BLK), bf16),
            pltpu.SMEM((N_DP,), jnp.int32),
            dma((12,)),
            dma((N_DP,)), dma((N_DP,)),
            dma((3,)), dma((3,)),
            dma((3,)), dma((3,)),
            dma((2, 4)), dma((2, 4)),
            dma((2, 4)), dma((2, 4)),
            dma((2, 4, 8)), dma((2, 4, 8)),
            dma((2,)), dma((2,)),
            dma((2,)), dma((2,)),
            dma((4, N_DP)), dma((4, N_DP)),
            dma,
        ],
        compiler_params=pltpu.CompilerParams(
            collective_id=0, has_side_effects=True, vmem_limit_bytes=63 * 1024 * 1024
        ),
        name="kfac",
    )(owners, counts, acts, grads_out, bases_a, bases_g.reshape(BLK, BLK))
    return pl.pallas_call(
        order_kernel,
        out_shape=jax.ShapeDtypeStruct((8, 4, 32, BLK), bf16),
        in_specs=[smem, hbm],
        out_specs=hbm,
        scratch_shapes=[dma((N_DP,))],
        name="order",
    )(owners, pieces)


def solution(mesh):
    placed = (
        P(None, "dp", None),
        P(None, "dp", "mp"),
        P(),
        P(),
        P(None, "mp", None),
        P("mp", "dp", None, None),
    )
    return jax.shard_map(
        local, mesh=mesh, in_specs=placed, out_specs=P(None, "mp", "dp", None), check_vma=False
    )
```

```python
import functools

import jax
import jax.numpy as jnp
from jax import lax
from jax.experimental import pallas as pl
from jax.experimental.pallas import tpu as pltpu
from jax.sharding import PartitionSpec as P

MESH = pl.DeviceIdType.MESH
damping = 0.0001
BLK = 1024
TILE = 256
HCOL = 512
NY, NX, NC, NZ = 4, 4, 2, 4
N_DP = NY * NX * NC
HALF = 64
SUB = HALF // NZ

PAIRS = [(2, 2), (1, 3), (3, 1), (2, 0), (0, 2), (1, 1), (3, 3), (2, 1), (2, 3), (1, 2), (3, 2), (0, 1), (1, 0), (0, 3), (3, 0)]
SPREAD = [(dy, dx, dc) for dc in range(NC) for dy, dx in PAIRS] + [(0, 0, 1)]
SLOTS = (1, 3, 2)
SECOND = [(0, 0), (0, 1), (2, 0), (2, 1), (1, 0), (3, 0), (1, 1), (3, 1)]
COLS = 256


def kernel(
    own_ref, cnt_ref, acts_hbm, grads_hbm, ba_hbm, bg_hbm, out_hbm,
    graw, araw, baraw, bg, first, mid, rows, sa, ra, proj, basis, lam, lam_g, cross, mask, inv_ref,
    load_sem, act_send, act_recv, ba_send, ba_recv, lam_send, lam_recv,
    p1_send, p1_recv, p1e_send, p1e_recv, p2_send, p2_recv, z_send, z_recv, out_send, out_recv, store_sem,
):
    me, mz = lax.axis_index("dp"), lax.axis_index("mp")
    my, mx, mc = me // 8, (me // 2) % 4, me % 2

    def at(dy, dx, dc):
        return ((my + dy) % NY) * 8 + ((mx + dx) % NX) * 2 + (mc + dc) % NC

    def zat(dz):
        return (me, (mz + dz) % NZ)

    def send(src, dst, ssem, rsem, target):
        copy = pltpu.make_async_remote_copy(
            src_ref=src, dst_ref=dst, send_sem=ssem, recv_sem=rsem, device_id=target, device_id_type=MESH
        )
        copy.start()
        return copy

    loads = [
        pltpu.make_async_copy(acts_hbm.at[:, pl.ds(mz * SUB, SUB)], araw.at[:, 0], load_sem.at[0]),
        pltpu.make_async_copy(acts_hbm.at[:, pl.ds(HALF + mz * SUB, SUB)], araw.at[:, 1], load_sem.at[1]),
    ]
    for j in range(8):
        loads.append(
            pltpu.make_async_copy(grads_hbm.at[:, :, pl.ds(j * HCOL, HCOL)], graw.at[j], load_sem.at[2 + j])
        )
    loads.append(pltpu.make_async_copy(ba_hbm, baraw, load_sem.at[10]))
    loads.append(pltpu.make_async_copy(bg_hbm, bg, load_sem.at[11]))
    for copy in loads:
        copy.start()

    barrier = pltpu.get_barrier_semaphore()
    peers = [(at(*d), mz) for d in SPREAD] + [zat(dz) for dz in (1, 2, 3)]
    for peer in peers:
        pl.semaphore_signal(barrier, inc=1, device_id=peer, device_id_type=MESH)

    def invert(d, carry):
        unit = jnp.int32(0)
        for u in range(1, N_DP):
            unit = jnp.where(own_ref[u] == d, u, unit)
        inv_ref[d] = unit
        return carry

    lax.fori_loop(0, N_DP, invert, 0)

    live = cnt_ref[me] - HALF
    row_ids = lax.broadcasted_iota(jnp.int32, (HALF, BLK), 0)
    mask[...] = jnp.where(row_ids < live, 1.0, 0.0).astype(jnp.bfloat16)

    sub_mask = mask[pl.ds(pl.multiple_of(mz * SUB, SUB), SUB), :]

    def pack_acts(dst, index, disp):
        layer = inv_ref[at(*disp)] // 4
        dst[index, pl.ds(0, SUB), :] = araw[layer, 0]
        dst[index, pl.ds(SUB, SUB), :] = araw[layer, 1] * sub_mask

    def index_of(dy, dx, dc):
        return (dy * 4 + dx) * 2 + dc

    loads[0].wait()
    loads[1].wait()
    for disp in SPREAD:
        pack_acts(sa, index_of(*disp), disp)
    pack_acts(ra, 0, (0, 0, 0))

    def disp_of(half, slot, e):
        other, dc = SECOND[e]
        return (other, slot, dc) if half == 0 else (slot, other, dc)

    def hop(half, slot):
        return (at(0, slot, 0) if half == 0 else at(slot, 0, 0), mz)

    def pack(dst, half, disp):
        unit = inv_ref[at(*disp)]
        layer, column = unit // 4, unit % 4
        for c in range(2):
            cols = pl.ds(c * HCOL, HCOL)
            block = graw[column * 2 + c, layer, pl.ds(half * HALF, HALF), :]
            dst[:, cols] = block if half == 0 else block * mask[:, cols]

    p1, p1e = {}, {}

    p2 = []

    def hop_two(half, slot, e, other, dc):
        return pltpu.make_async_remote_copy(
            src_ref=mid.at[half, slot, e - 1],
            dst_ref=rows.at[(half * 4 + slot) * 8 + e],
            send_sem=p2_send.at[half, slot, e],
            recv_sem=p2_recv.at[half, slot, e],
            device_id=(at(other, 0, dc) if half == 0 else at(0, other, dc), mz),
            device_id_type=MESH,
        )

    def forward(slot, core):
        dc = (core + mc) % 2
        for other in (2, 1, 3):
            e = jnp.where(dc == 0, SECOND.index((other, 0)), SECOND.index((other, 1)))
            for half in range(2):
                p2.append(hop_two(half, slot, e, other, dc))
                p2[-1].start()
        if core == 0:
            for half in range(2):
                p2.append(hop_two(half, slot, 1, 0, 1))
                p2[-1].start()

    def pack_slot(slot):
        for half in range(2):
            for e in range(8):
                pack(first.at[half, slot - 1, e], half, disp_of(half, slot, e))

    def start_slot(slot):
        for half in range(2):
            p1[half, slot] = send(
                first.at[half, slot - 1, pl.ds(1, 7)], mid.at[half, slot],
                p1_send.at[half, slot], p1_recv.at[half, slot], hop(half, slot),
            )
            p1e[half, slot] = send(
                first.at[half, slot - 1, 0], rows.at[(half * 4 + slot) * 8],
                p1e_send.at[half, slot], p1e_recv.at[half, slot], hop(half, slot),
            )

    for j in range(8):
        loads[2 + j].wait()
    for half in range(2):
        for e in range(1, 8):
            pack(mid.at[half, 0, e - 1], half, disp_of(half, 0, e))
        pack(rows.at[half * 32], half, disp_of(half, 0, 0))
    loads[10].wait()
    basis[mz] = baraw[inv_ref[me] // 4]

    pl.semaphore_wait(barrier, len(peers))
    act_copies = []
    for disp in SPREAD:
        i = index_of(*disp)
        act_copies.append(send(sa.at[i], ra.at[i], act_send.at[i], act_recv.at[i], (at(*disp), mz)))
    ba_copies = [
        send(basis.at[mz], basis.at[mz], ba_send.at[k], ba_recv.at[k], zat(dz)) for k, dz in enumerate(SLOTS)
    ]
    forward(0, 0)
    forward(0, 1)
    for slot in SLOTS:
        pack_slot(slot)
        start_slot(slot)

    loads[11].wait()
    for k in range(4):
        baraw[k] = jnp.transpose(bg[:, k * TILE : (k + 1) * TILE], (1, 0))

    for copy in act_copies:
        copy.wait_recv()
    for copy in ba_copies:
        copy.wait_recv()
    lam[mz] = jnp.zeros((8, BLK), jnp.float32)
    lam_g[...] = jnp.zeros_like(lam_g)
    cross[...] = jnp.zeros_like(cross)

    def proj_a_step(step, carry):
        block = ra[pl.ds(step * 16, 16)].reshape(512, BLK)
        value = jnp.dot(block, basis[...].reshape(BLK, BLK), preferred_element_type=jnp.float32)
        lam[mz] += jnp.sum((value * value).reshape(64, 8, BLK), axis=0)
        value = value.astype(jnp.bfloat16)
        for y in range(2):
            dy = step * 2 + y
            for dx in range(4):
                for dc in range(2):
                    r = (y * 8 + dx * 2 + dc) * 32
                    e = 2 * step + dc if y == 0 else 4 + step + 2 * dc
                    proj[dx * 8 + e, mz] = value[r : r + SUB]
                    proj[(4 + dy) * 8 + SECOND.index((dx, dc)), mz] = value[r + SUB : r + 2 * SUB]
        return carry

    lax.fori_loop(0, 2, proj_a_step, 0)

    z_copies = {}

    def z_send_half(slot, half, owner, k, target):
        piece = proj.at[pl.ds((half * 4 + slot) * 8, 8), owner]
        z_copies[slot, k] = send(piece, piece, z_send.at[slot, k], z_recv.at[slot, k], target)

    def z_start(slot):
        z_send_half(slot, 0, mz, 0, zat(1))
        z_send_half(slot, 1, mz, 1, zat(3))
        z_send_half(slot, 1, mz, 2, zat(1))
        z_send_half(slot, 0, mz, 3, zat(3))

    def z_forward(slot):
        z_copies[slot, 0].wait_recv()
        z_send_half(slot, 0, (mz + 3) % NZ, 4, zat(1))
        z_copies[slot, 1].wait_recv()
        z_send_half(slot, 1, (mz + 1) % NZ, 5, zat(3))

    z_start(0)
    lam_copies = [send(lam.at[mz], lam.at[mz], lam_send.at[k], lam_recv.at[k], zat(dz)) for k, dz in enumerate(SLOTS)]
    z_start(1)
    z_forward(0)
    z_start(3)
    z_forward(1)
    z_start(2)

    def take_slot(slot):
        for half in range(2):
            p1[half, slot].wait_recv()
        forward(slot, 0)
        if slot == 1:
            forward(slot, 1)

    take_slot(1)
    z_forward(3)
    take_slot(3)
    take_slot(2)
    forward(3, 1)
    forward(2, 1)
    z_forward(2)

    def arrived(half, slot, blocks):
        for e in blocks:
            if slot == 0 and e == 0:
                continue
            (p1e[half, slot] if e == 0 else hop_two(half, slot, e, *SECOND[e])).wait_recv()

    def project(block):
        value = lax.dot_general(
            baraw[pl.ds(0, 4)].reshape(BLK, BLK), block, (((1,), (1,)), ((), ())), preferred_element_type=jnp.float32
        )
        square = value * value
        part = square[:, 0:128]
        for k in range(1, block.shape[0] // 128):
            part += square[:, k * 128 : (k + 1) * 128]
        lam_g[...] += part
        return value.astype(jnp.bfloat16)

    def proj_g(slot, count):
        def step(half, carry):
            g = half * 4 + slot
            value = project(rows[pl.ds(g * 8, count)].reshape(count * HALF, BLK))
            graw[g, :, :, pl.ds(0, count * HALF)] = value.reshape(8, 128, count * HALF)
            return carry

        for half in range(2):
            arrived(half, slot, range(count))
        lax.fori_loop(0, 2, step, 0)

    def add_cross(slot, count):
        def step(i, carry):
            half, part = i // 2, i % 2
            g = half * 4 + slot
            right = proj[pl.ds(g * 8, count)].reshape(count * HALF, BLK)
            left = graw[g, pl.ds(part * 4, 4), :, pl.ds(0, count * HALF)].reshape(512, count * HALF)
            prows = pl.ds(pl.multiple_of(part * 512, 512), 512)
            cross[prows, :] += jnp.dot(left, right, preferred_element_type=jnp.float32)
            return carry

        lax.fori_loop(0, 4, step, 0)

    def z_arrived(slot):
        for k in range(2, 6):
            z_copies[slot, k].wait_recv()

    for slot in (0, 1, 3):
        proj_g(slot, 8)
        z_arrived(slot)
        add_cross(slot, 8)
    proj_g(2, 4)
    z_arrived(2)
    add_cross(2, 4)

    def pair(e):
        for half in range(2):
            arrived(half, 2, (e, e + 1))
        starts = [(half * 4 + 2) * 8 + e for half in range(2)]
        block = jnp.concatenate([rows[b : b + 2].reshape(128, BLK) for b in starts], axis=0)
        right = jnp.concatenate([proj[b : b + 2].reshape(128, BLK) for b in starts], axis=0)
        return project(block), right

    pair_g, pair_a = pair(4)
    for part in range(2):
        prows = slice(part * 512, part * 512 + 512)
        cross[prows, :] += jnp.dot(pair_g[prows], pair_a, preferred_element_type=jnp.float32)
    last_g, last_a = pair(6)

    for copy in lam_copies:
        copy.wait_recv()
    total = cnt_ref[0]
    for s in range(1, N_DP):
        total += cnt_ref[s]
    row_total = total.astype(jnp.float32)
    row_a = jnp.sum(lam[0] + lam[1] + lam[2] + lam[3], axis=0, keepdims=True) / row_total
    col_g = jnp.sum(lam_g[...], axis=1, keepdims=True) / row_total
    for part in range(2):
        prows = slice(part * 512, part * 512 + 512)
        value = cross[prows, :] + jnp.dot(last_g[prows], last_a, preferred_element_type=jnp.float32)
        scaled = (value / row_total) / (col_g[prows] * row_a + damping)
        baraw[4 + part * 2 : 6 + part * 2] = scaled.astype(jnp.bfloat16).reshape(2, 256, BLK)

    for copies in (act_copies, p1.values(), p1e.values()):
        for copy in copies:
            copy.wait_send()

    out_copies = []
    for part in range(4):
        prows, cols = pl.ds(part * COLS, COLS), pl.ds(part * COLS, COLS)
        right = jnp.dot(
            bg[prows, :], baraw[pl.ds(4, 4)].reshape(BLK, BLK), preferred_element_type=jnp.float32
        ).astype(jnp.bfloat16)
        sa[:, :, cols] = lax.dot_general(
            basis[...].reshape(BLK, BLK), right, (((1,), (1,)), ((), ())), preferred_element_type=jnp.float32
        ).astype(jnp.bfloat16).reshape(N_DP, 32, COLS)
        for disp in SPREAD:
            i, target = index_of(*disp), at(*disp)
            out_copies.append(
                send(
                    sa.at[target, :, cols], out_hbm.at[me, :, cols],
                    out_send.at[part, i], out_recv.at[part, i], (target, mz),
                )
            )
    own = pltpu.make_async_copy(sa.at[me], out_hbm.at[me], store_sem)
    own.start()
    for copy in out_copies:
        copy.wait_recv()
    own.wait()
    for copy in out_copies + ba_copies + lam_copies + list(z_copies.values()) + p2:
        copy.wait_send()


def order_kernel(own_ref, pieces_hbm, out_hbm, held, load_sem, store_sem):
    loads = [pltpu.make_async_copy(pieces_hbm.at[own_ref[u]], held.at[u], load_sem.at[u]) for u in range(N_DP)]
    for copy in loads:
        copy.start()
    stores = []
    for layer in range(8):
        for copy in loads[layer * 4 : layer * 4 + 4]:
            copy.wait()
        stores.append(pltpu.make_async_copy(held.at[pl.ds(layer * 4, 4)], out_hbm.at[layer], store_sem.at[layer]))
        stores[-1].start()
    for copy in stores:
        copy.wait()


def local(acts, grads_out, counts, owners, bases_a, bases_g):
    smem = pl.BlockSpec(memory_space=pltpu.SMEM)
    hbm = pl.BlockSpec(memory_space=pl.ANY)
    bf16, f32 = jnp.bfloat16, jnp.float32
    dma = pltpu.SemaphoreType.DMA
    pieces = pl.pallas_call(
        kernel,
        out_shape=jax.ShapeDtypeStruct((N_DP, 32, BLK), bf16),
        in_specs=[smem, smem, hbm, hbm, hbm, hbm],
        out_specs=hbm,
        scratch_shapes=[
            pltpu.VMEM((8, 8, 128, HCOL), bf16),
            pltpu.VMEM((8, 2, SUB, BLK), bf16),
            pltpu.VMEM((8, 256, BLK), bf16),
            pltpu.VMEM((BLK, BLK), bf16),
            pltpu.VMEM((2, 3, 8, HALF, BLK), bf16),
            pltpu.VMEM((2, 4, 7, HALF, BLK), bf16),
            pltpu.VMEM((64, HALF, BLK), bf16),
            pltpu.VMEM((N_DP, 32, BLK), bf16),
            pltpu.VMEM((N_DP, 32, BLK), bf16),
            pltpu.VMEM((64, NZ, SUB, BLK), bf16),
            pltpu.VMEM((NZ, 256, BLK), bf16),
            pltpu.VMEM((NZ, 8, BLK), f32),
            pltpu.VMEM((BLK, 128), f32),
            pltpu.VMEM((BLK, BLK), f32),
            pltpu.VMEM((HALF, BLK), bf16),
            pltpu.SMEM((N_DP,), jnp.int32),
            dma((12,)),
            dma((N_DP,)), dma((N_DP,)),
            dma((3,)), dma((3,)),
            dma((3,)), dma((3,)),
            dma((2, 4)), dma((2, 4)),
            dma((2, 4)), dma((2, 4)),
            dma((2, 4, 8)), dma((2, 4, 8)),
            dma((4, 6)), dma((4, 6)),
            dma((4, N_DP)), dma((4, N_DP)),
            dma,
        ],
        compiler_params=pltpu.CompilerParams(
            collective_id=0, has_side_effects=True, vmem_limit_bytes=63 * 1024 * 1024
        ),
        name="kfac",
    )(owners, counts, acts, grads_out, bases_a, bases_g.reshape(BLK, BLK))
    return pl.pallas_call(
        order_kernel,
        out_shape=jax.ShapeDtypeStruct((8, 4, 32, BLK), bf16),
        in_specs=[smem, hbm],
        out_specs=hbm,
        scratch_shapes=[pltpu.VMEM((N_DP, 32, BLK), bf16), dma((N_DP,)), dma((8,))],
        name="order",
    )(owners, pieces)


def solution(mesh):
    placed = (
        P(None, "dp", None),
        P(None, "dp", "mp"),
        P(),
        P(),
        P(None, "mp", None),
        P("mp", "dp", None, None),
    )
    return jax.shard_map(
        local, mesh=mesh, in_specs=placed, out_specs=P(None, "mp", "dp", None), check_vma=False
    )
```

```python
import functools

import jax
import jax.numpy as jnp
from jax import lax
from jax.experimental import pallas as pl
from jax.experimental.pallas import tpu as pltpu
from jax.sharding import PartitionSpec as P

MESH = pl.DeviceIdType.MESH
damping = 0.0001
BLK = 1024
TILE = 256
HCOL = 512
NY, NX, NC, NZ = 4, 4, 2, 4
N_DP = NY * NX * NC
HALF = 64
SUB = HALF // NZ

PAIRS = [(2, 2), (1, 3), (3, 1), (2, 0), (0, 2), (1, 1), (3, 3), (2, 1), (2, 3), (1, 2), (3, 2), (0, 1), (1, 0), (0, 3), (3, 0)]
SPREAD = [(dy, dx, dc) for dc in range(NC) for dy, dx in PAIRS] + [(0, 0, 1)]
SLOTS = (1, 3, 2)
SECOND = [(0, 0), (0, 1), (2, 0), (2, 1), (1, 0), (3, 0), (1, 1), (3, 1)]
COLS = 256


def kernel(
    own_ref, cnt_ref, acts_hbm, grads_hbm, ba_hbm, bg_hbm, out_hbm,
    graw, araw, baraw, bg, first, mid, rows, sa, ra, proj, basis, lam, lam_g, cross, mask, inv_ref,
    load_sem, act_send, act_recv, ba_send, ba_recv, lam_send, lam_recv,
    p1_send, p1_recv, p1e_send, p1e_recv, p2_send, p2_recv, z_send, z_recv, out_send, out_recv, store_sem,
):
    me, mz = lax.axis_index("dp"), lax.axis_index("mp")
    my, mx, mc = me // 8, (me // 2) % 4, me % 2

    def at(dy, dx, dc):
        return ((my + dy) % NY) * 8 + ((mx + dx) % NX) * 2 + (mc + dc) % NC

    def zat(dz):
        return (me, (mz + dz) % NZ)

    def send(src, dst, ssem, rsem, target):
        copy = pltpu.make_async_remote_copy(
            src_ref=src, dst_ref=dst, send_sem=ssem, recv_sem=rsem, device_id=target, device_id_type=MESH
        )
        copy.start()
        return copy

    barrier = pltpu.get_barrier_semaphore()
    peers = [(at(*d), mz) for d in SPREAD] + [zat(dz) for dz in (1, 2, 3)]
    for peer in peers:
        pl.semaphore_signal(barrier, inc=1, device_id=peer, device_id_type=MESH)

    loads = [
        pltpu.make_async_copy(acts_hbm.at[:, pl.ds(mz * SUB, SUB)], araw.at[:, 0], load_sem.at[0]),
        pltpu.make_async_copy(acts_hbm.at[:, pl.ds(HALF + mz * SUB, SUB)], araw.at[:, 1], load_sem.at[1]),
    ]
    loads.append(pltpu.make_async_copy(ba_hbm, baraw, load_sem.at[10]))
    for j in range(8):
        loads.append(
            pltpu.make_async_copy(grads_hbm.at[:, :, pl.ds(j * HCOL, HCOL)], graw.at[j], load_sem.at[2 + j])
        )
    loads.append(pltpu.make_async_copy(bg_hbm, bg, load_sem.at[11]))
    for copy in loads:
        copy.start()

    def invert(d, carry):
        unit = jnp.int32(0)
        for u in range(1, N_DP):
            unit = jnp.where(own_ref[u] == d, u, unit)
        inv_ref[d] = unit
        return carry

    lax.fori_loop(0, N_DP, invert, 0)

    live = cnt_ref[me] - HALF
    row_ids = lax.broadcasted_iota(jnp.int32, (HALF, BLK), 0)
    mask[...] = jnp.where(row_ids < live, 1.0, 0.0).astype(jnp.bfloat16)

    sub_mask = mask[pl.ds(pl.multiple_of(mz * SUB, SUB), SUB), :]

    def pack_acts(dst, index, disp):
        layer = inv_ref[at(*disp)] // 4
        dst[index, pl.ds(0, SUB), :] = araw[layer, 0]
        dst[index, pl.ds(SUB, SUB), :] = araw[layer, 1] * sub_mask

    def index_of(dy, dx, dc):
        return (dy * 4 + dx) * 2 + dc

    loads[0].wait()
    loads[1].wait()
    for disp in SPREAD:
        pack_acts(sa, index_of(*disp), disp)
    pack_acts(ra, 0, (0, 0, 0))

    pl.semaphore_wait(barrier, len(peers))
    act_copies = []
    for disp in SPREAD:
        i = index_of(*disp)
        act_copies.append(send(sa.at[i], ra.at[i], act_send.at[i], act_recv.at[i], (at(*disp), mz)))

    loads[2].wait()
    basis[mz] = baraw[inv_ref[me] // 4]
    ba_copies = [
        send(basis.at[mz], basis.at[mz], ba_send.at[k], ba_recv.at[k], zat(dz)) for k, dz in enumerate(SLOTS)
    ]

    def disp_of(half, slot, e):
        other, dc = SECOND[e]
        return (other, slot, dc) if half == 0 else (slot, other, dc)

    def hop(half, slot):
        return (at(0, slot, 0) if half == 0 else at(slot, 0, 0), mz)

    def pack(dst, half, disp):
        unit = inv_ref[at(*disp)]
        layer, column = unit // 4, unit % 4
        for c in range(2):
            cols = pl.ds(c * HCOL, HCOL)
            block = graw[column * 2 + c, layer, pl.ds(half * HALF, HALF), :]
            dst[:, cols] = block if half == 0 else block * mask[:, cols]

    p1, p1e = {}, {}

    p2 = []

    def hop_two(half, slot, e, other, dc):
        return pltpu.make_async_remote_copy(
            src_ref=mid.at[half, slot, e - 1],
            dst_ref=rows.at[(half * 4 + slot) * 8 + e],
            send_sem=p2_send.at[half, slot, e],
            recv_sem=p2_recv.at[half, slot, e],
            device_id=(at(other, 0, dc) if half == 0 else at(0, other, dc), mz),
            device_id_type=MESH,
        )

    def forward(slot, core):
        dc = (core + mc) % 2
        for other in (2, 1, 3):
            e = jnp.where(dc == 0, SECOND.index((other, 0)), SECOND.index((other, 1)))
            for half in range(2):
                p2.append(hop_two(half, slot, e, other, dc))
                p2[-1].start()
        if core == 0:
            for half in range(2):
                p2.append(hop_two(half, slot, 1, 0, 1))
                p2[-1].start()

    def pack_slot(slot):
        for half in range(2):
            for e in range(8):
                pack(first.at[half, slot - 1, e], half, disp_of(half, slot, e))

    def start_slot(slot):
        for half in range(2):
            p1[half, slot] = send(
                first.at[half, slot - 1, pl.ds(1, 7)], mid.at[half, slot],
                p1_send.at[half, slot], p1_recv.at[half, slot], hop(half, slot),
            )
            p1e[half, slot] = send(
                first.at[half, slot - 1, 0], rows.at[(half * 4 + slot) * 8],
                p1e_send.at[half, slot], p1e_recv.at[half, slot], hop(half, slot),
            )

    for j in range(8):
        loads[3 + j].wait()
    for half in range(2):
        for e in range(1, 8):
            pack(mid.at[half, 0, e - 1], half, disp_of(half, 0, e))
        pack(rows.at[half * 32], half, disp_of(half, 0, 0))
    forward(0, 0)
    forward(0, 1)
    for slot in SLOTS:
        pack_slot(slot)
        start_slot(slot)

    loads[11].wait()
    for k in range(4):
        baraw[k] = jnp.transpose(bg[:, k * TILE : (k + 1) * TILE], (1, 0))

    for copy in act_copies:
        copy.wait_recv()
    for copy in ba_copies:
        copy.wait_recv()
    lam[mz] = jnp.zeros((8, BLK), jnp.float32)
    lam_g[...] = jnp.zeros_like(lam_g)
    cross[...] = jnp.zeros_like(cross)

    def proj_a_step(step, carry):
        block = ra[pl.ds(step * 16, 16)].reshape(512, BLK)
        value = jnp.dot(block, basis[...].reshape(BLK, BLK), preferred_element_type=jnp.float32)
        lam[mz] += jnp.sum((value * value).reshape(64, 8, BLK), axis=0)
        value = value.astype(jnp.bfloat16)
        for y in range(2):
            dy = step * 2 + y
            for dx in range(4):
                for dc in range(2):
                    r = (y * 8 + dx * 2 + dc) * 32
                    e = 2 * step + dc if y == 0 else 4 + step + 2 * dc
                    proj[dx * 8 + e, mz] = value[r : r + SUB]
                    proj[(4 + dy) * 8 + SECOND.index((dx, dc)), mz] = value[r + SUB : r + 2 * SUB]
        return carry

    lax.fori_loop(0, 2, proj_a_step, 0)

    z_copies = {}

    def z_send_half(slot, half, owner, k, target):
        piece = proj.at[pl.ds((half * 4 + slot) * 8, 8), owner]
        z_copies[slot, k] = send(piece, piece, z_send.at[slot, k], z_recv.at[slot, k], target)

    def z_start(slot):
        z_send_half(slot, 0, mz, 0, zat(1))
        z_send_half(slot, 1, mz, 1, zat(3))
        z_send_half(slot, 1, mz, 2, zat(1))
        z_send_half(slot, 0, mz, 3, zat(3))

    def z_forward(slot):
        z_copies[slot, 0].wait_recv()
        z_send_half(slot, 0, (mz + 3) % NZ, 4, zat(1))
        z_copies[slot, 1].wait_recv()
        z_send_half(slot, 1, (mz + 1) % NZ, 5, zat(3))

    z_start(0)
    lam_copies = [send(lam.at[mz], lam.at[mz], lam_send.at[k], lam_recv.at[k], zat(dz)) for k, dz in enumerate(SLOTS)]
    z_start(1)
    z_forward(0)
    z_start(3)
    z_forward(1)
    z_start(2)

    def take_slot(slot):
        for half in range(2):
            p1[half, slot].wait_recv()
        forward(slot, 0)


    take_slot(1)
    z_forward(3)
    take_slot(3)
    take_slot(2)
    forward(1, 1)
    forward(3, 1)
    forward(2, 1)
    z_forward(2)

    def arrived(half, slot, blocks):
        for e in blocks:
            if slot == 0 and e == 0:
                continue
            (p1e[half, slot] if e == 0 else hop_two(half, slot, e, *SECOND[e])).wait_recv()

    def project(block):
        value = lax.dot_general(
            baraw[pl.ds(0, 4)].reshape(BLK, BLK), block, (((1,), (1,)), ((), ())), preferred_element_type=jnp.float32
        )
        square = value * value
        part = square[:, 0:128]
        for k in range(1, block.shape[0] // 128):
            part += square[:, k * 128 : (k + 1) * 128]
        lam_g[...] += part
        return value.astype(jnp.bfloat16)

    def proj_g(slot, count):
        def step(half, carry):
            g = half * 4 + slot
            value = project(rows[pl.ds(g * 8, count)].reshape(count * HALF, BLK))
            graw[g, :, :, pl.ds(0, count * HALF)] = value.reshape(8, 128, count * HALF)
            return carry

        for half in range(2):
            arrived(half, slot, range(count))
        lax.fori_loop(0, 2, step, 0)

    def add_cross(slot, count):
        def step(i, carry):
            half, part = i // 2, i % 2
            g = half * 4 + slot
            right = proj[pl.ds(g * 8, count)].reshape(count * HALF, BLK)
            left = graw[g, pl.ds(part * 4, 4), :, pl.ds(0, count * HALF)].reshape(512, count * HALF)
            prows = pl.ds(pl.multiple_of(part * 512, 512), 512)
            cross[prows, :] += jnp.dot(left, right, preferred_element_type=jnp.float32)
            return carry

        lax.fori_loop(0, 4, step, 0)

    def z_arrived(slot):
        for k in range(2, 6):
            z_copies[slot, k].wait_recv()

    for slot in (0, 1, 3):
        proj_g(slot, 8)
        z_arrived(slot)
        add_cross(slot, 8)
    proj_g(2, 4)
    z_arrived(2)
    add_cross(2, 4)

    def pair(e):
        for half in range(2):
            arrived(half, 2, (e, e + 1))
        starts = [(half * 4 + 2) * 8 + e for half in range(2)]
        block = jnp.concatenate([rows[b : b + 2].reshape(128, BLK) for b in starts], axis=0)
        right = jnp.concatenate([proj[b : b + 2].reshape(128, BLK) for b in starts], axis=0)
        return project(block), right

    pair_g, pair_a = pair(4)
    for part in range(2):
        prows = slice(part * 512, part * 512 + 512)
        cross[prows, :] += jnp.dot(pair_g[prows], pair_a, preferred_element_type=jnp.float32)
    last_g, last_a = pair(6)

    for copy in lam_copies:
        copy.wait_recv()
    total = cnt_ref[0]
    for s in range(1, N_DP):
        total += cnt_ref[s]
    row_total = total.astype(jnp.float32)
    row_a = jnp.sum(lam[0] + lam[1] + lam[2] + lam[3], axis=0, keepdims=True) / row_total
    col_g = jnp.sum(lam_g[...], axis=1, keepdims=True) / row_total
    for part in range(2):
        prows = slice(part * 512, part * 512 + 512)
        value = cross[prows, :] + jnp.dot(last_g[prows], last_a, preferred_element_type=jnp.float32)
        scaled = (value / row_total) / (col_g[prows] * row_a + damping)
        baraw[4 + part * 2 : 6 + part * 2] = scaled.astype(jnp.bfloat16).reshape(2, 256, BLK)

    for copies in (act_copies, p1.values(), p1e.values()):
        for copy in copies:
            copy.wait_send()

    out_copies = []
    for part in range(4):
        prows, cols = pl.ds(part * COLS, COLS), pl.ds(part * COLS, COLS)
        right = jnp.dot(
            bg[prows, :], baraw[pl.ds(4, 4)].reshape(BLK, BLK), preferred_element_type=jnp.float32
        ).astype(jnp.bfloat16)
        sa[:, :, cols] = lax.dot_general(
            basis[...].reshape(BLK, BLK), right, (((1,), (1,)), ((), ())), preferred_element_type=jnp.float32
        ).astype(jnp.bfloat16).reshape(N_DP, 32, COLS)
        for disp in SPREAD:
            i, target = index_of(*disp), at(*disp)
            out_copies.append(
                send(
                    sa.at[target, :, cols], out_hbm.at[me, :, cols],
                    out_send.at[part, i], out_recv.at[part, i], (target, mz),
                )
            )
    own = pltpu.make_async_copy(sa.at[me], out_hbm.at[me], store_sem)
    own.start()
    for copy in out_copies:
        copy.wait_recv()
    own.wait()
    for copy in out_copies + ba_copies + lam_copies + list(z_copies.values()) + p2:
        copy.wait_send()


def order_kernel(own_ref, pieces_hbm, out_hbm, held, load_sem, store_sem):
    loads = [pltpu.make_async_copy(pieces_hbm.at[own_ref[u]], held.at[u], load_sem.at[u]) for u in range(N_DP)]
    for copy in loads:
        copy.start()
    stores = []
    for layer in range(8):
        for copy in loads[layer * 4 : layer * 4 + 4]:
            copy.wait()
        stores.append(pltpu.make_async_copy(held.at[pl.ds(layer * 4, 4)], out_hbm.at[layer], store_sem.at[layer]))
        stores[-1].start()
    for copy in stores:
        copy.wait()


def local(acts, grads_out, counts, owners, bases_a, bases_g):
    smem = pl.BlockSpec(memory_space=pltpu.SMEM)
    hbm = pl.BlockSpec(memory_space=pl.ANY)
    bf16, f32 = jnp.bfloat16, jnp.float32
    dma = pltpu.SemaphoreType.DMA
    pieces = pl.pallas_call(
        kernel,
        out_shape=jax.ShapeDtypeStruct((N_DP, 32, BLK), bf16),
        in_specs=[smem, smem, hbm, hbm, hbm, hbm],
        out_specs=hbm,
        scratch_shapes=[
            pltpu.VMEM((8, 8, 128, HCOL), bf16),
            pltpu.VMEM((8, 2, SUB, BLK), bf16),
            pltpu.VMEM((8, 256, BLK), bf16),
            pltpu.VMEM((BLK, BLK), bf16),
            pltpu.VMEM((2, 3, 8, HALF, BLK), bf16),
            pltpu.VMEM((2, 4, 7, HALF, BLK), bf16),
            pltpu.VMEM((64, HALF, BLK), bf16),
            pltpu.VMEM((N_DP, 32, BLK), bf16),
            pltpu.VMEM((N_DP, 32, BLK), bf16),
            pltpu.VMEM((64, NZ, SUB, BLK), bf16),
            pltpu.VMEM((NZ, 256, BLK), bf16),
            pltpu.VMEM((NZ, 8, BLK), f32),
            pltpu.VMEM((BLK, 128), f32),
            pltpu.VMEM((BLK, BLK), f32),
            pltpu.VMEM((HALF, BLK), bf16),
            pltpu.SMEM((N_DP,), jnp.int32),
            dma((12,)),
            dma((N_DP,)), dma((N_DP,)),
            dma((3,)), dma((3,)),
            dma((3,)), dma((3,)),
            dma((2, 4)), dma((2, 4)),
            dma((2, 4)), dma((2, 4)),
            dma((2, 4, 8)), dma((2, 4, 8)),
            dma((4, 6)), dma((4, 6)),
            dma((4, N_DP)), dma((4, N_DP)),
            dma,
        ],
        compiler_params=pltpu.CompilerParams(
            collective_id=0, has_side_effects=True, vmem_limit_bytes=63 * 1024 * 1024
        ),
        name="kfac",
    )(owners, counts, acts, grads_out, bases_a, bases_g.reshape(BLK, BLK))
    return pl.pallas_call(
        order_kernel,
        out_shape=jax.ShapeDtypeStruct((8, 4, 32, BLK), bf16),
        in_specs=[smem, hbm],
        out_specs=hbm,
        scratch_shapes=[pltpu.VMEM((N_DP, 32, BLK), bf16), dma((N_DP,)), dma((8,))],
        name="order",
    )(owners, pieces)


def solution(mesh):
    placed = (
        P(None, "dp", None),
        P(None, "dp", "mp"),
        P(),
        P(),
        P(None, "mp", None),
        P("mp", "dp", None, None),
    )
    return jax.shard_map(
        local, mesh=mesh, in_specs=placed, out_specs=P(None, "mp", "dp", None), check_vma=False
    )
```

```python
import functools

import jax
import jax.numpy as jnp
from jax import lax
from jax.experimental import pallas as pl
from jax.experimental.pallas import tpu as pltpu
from jax.sharding import PartitionSpec as P

MESH = pl.DeviceIdType.MESH
damping = 0.0001
BLK = 1024
TILE = 256
HCOL = 512
NY, NX, NC, NZ = 4, 4, 2, 4
N_DP = NY * NX * NC
HALF = 64
SUB = HALF // NZ

PAIRS = [(2, 2), (1, 3), (3, 1), (2, 0), (0, 2), (1, 1), (3, 3), (2, 1), (2, 3), (1, 2), (3, 2), (0, 1), (1, 0), (0, 3), (3, 0)]
SPREAD = [(dy, dx, dc) for dc in range(NC) for dy, dx in PAIRS] + [(0, 0, 1)]
SLOTS = (1, 3, 2)
SECOND = [(0, 0), (0, 1), (2, 0), (2, 1), (1, 0), (3, 0), (1, 1), (3, 1)]
COLS = 256


def kernel(
    own_ref, cnt_ref, acts_hbm, grads_hbm, ba_hbm, bg_hbm, out_hbm,
    graw, araw, baraw, bg, first, mid, rows, sa, ra, proj, basis, lam, lam_g, cross, mask, inv_ref,
    load_sem, act_send, act_recv, ba_send, ba_recv, lam_send, lam_recv,
    p1_send, p1_recv, p1e_send, p1e_recv, p2_send, p2_recv, z_send, z_recv, out_send, out_recv, store_sem,
):
    me, mz = lax.axis_index("dp"), lax.axis_index("mp")
    my, mx, mc = me // 8, (me // 2) % 4, me % 2

    def at(dy, dx, dc):
        return ((my + dy) % NY) * 8 + ((mx + dx) % NX) * 2 + (mc + dc) % NC

    def zat(dz):
        return (me, (mz + dz) % NZ)

    def send(src, dst, ssem, rsem, target):
        copy = pltpu.make_async_remote_copy(
            src_ref=src, dst_ref=dst, send_sem=ssem, recv_sem=rsem, device_id=target, device_id_type=MESH
        )
        copy.start()
        return copy

    barrier = pltpu.get_barrier_semaphore()
    peers = [(at(*d), mz) for d in SPREAD] + [zat(dz) for dz in (1, 2, 3)]
    for peer in peers:
        pl.semaphore_signal(barrier, inc=1, device_id=peer, device_id_type=MESH)

    loads = [
        pltpu.make_async_copy(acts_hbm.at[:, pl.ds(mz * SUB, SUB)], araw.at[:, 0], load_sem.at[0]),
        pltpu.make_async_copy(acts_hbm.at[:, pl.ds(HALF + mz * SUB, SUB)], araw.at[:, 1], load_sem.at[1]),
    ]
    loads.append(pltpu.make_async_copy(ba_hbm, baraw, load_sem.at[10]))
    for j in range(8):
        loads.append(
            pltpu.make_async_copy(grads_hbm.at[:, :, pl.ds(j * HCOL, HCOL)], graw.at[j], load_sem.at[2 + j])
        )
    loads.append(pltpu.make_async_copy(bg_hbm, bg, load_sem.at[11]))
    for copy in loads:
        copy.start()

    def invert(d, carry):
        unit = jnp.int32(0)
        for u in range(1, N_DP):
            unit = jnp.where(own_ref[u] == d, u, unit)
        inv_ref[d] = unit
        return carry

    lax.fori_loop(0, N_DP, invert, 0)

    live = cnt_ref[me] - HALF
    row_ids = lax.broadcasted_iota(jnp.int32, (HALF, BLK), 0)
    mask[...] = jnp.where(row_ids < live, 1.0, 0.0).astype(jnp.bfloat16)

    sub_mask = mask[pl.ds(pl.multiple_of(mz * SUB, SUB), SUB), :]

    def pack_acts(dst, index, disp):
        layer = inv_ref[at(*disp)] // 4
        dst[index, pl.ds(0, SUB), :] = araw[layer, 0]
        dst[index, pl.ds(SUB, SUB), :] = araw[layer, 1] * sub_mask

    def index_of(dy, dx, dc):
        return (dy * 4 + dx) * 2 + dc

    loads[0].wait()
    loads[1].wait()
    for disp in SPREAD:
        pack_acts(sa, index_of(*disp), disp)
    pack_acts(ra, 0, (0, 0, 0))

    pl.semaphore_wait(barrier, len(peers))
    act_copies = []
    for disp in SPREAD:
        i = index_of(*disp)
        act_copies.append(send(sa.at[i], ra.at[i], act_send.at[i], act_recv.at[i], (at(*disp), mz)))

    loads[2].wait()
    basis[mz] = baraw[inv_ref[me] // 4]
    ba_copies = [
        send(basis.at[mz], basis.at[mz], ba_send.at[k], ba_recv.at[k], zat(dz)) for k, dz in enumerate(SLOTS)
    ]

    def disp_of(half, slot, e):
        other, dc = SECOND[e]
        return (other, slot, dc) if half == 0 else (slot, other, dc)

    def hop(half, slot):
        return (at(0, slot, 0) if half == 0 else at(slot, 0, 0), mz)

    def pack(dst, half, disp):
        unit = inv_ref[at(*disp)]
        layer, column = unit // 4, unit % 4
        for c in range(2):
            cols = pl.ds(c * HCOL, HCOL)
            block = graw[column * 2 + c, layer, pl.ds(half * HALF, HALF), :]
            dst[:, cols] = block if half == 0 else block * mask[:, cols]

    p1, p1e = {}, {}

    p2 = []

    def hop_two(half, slot, e, other, dc):
        return pltpu.make_async_remote_copy(
            src_ref=mid.at[half, slot, e - 1],
            dst_ref=rows.at[(half * 4 + slot) * 8 + e],
            send_sem=p2_send.at[half, slot, e],
            recv_sem=p2_recv.at[half, slot, e],
            device_id=(at(other, 0, dc) if half == 0 else at(0, other, dc), mz),
            device_id_type=MESH,
        )

    def forward(slot, core):
        dc = (core + mc) % 2
        for other in (2, 1, 3):
            e = jnp.where(dc == 0, SECOND.index((other, 0)), SECOND.index((other, 1)))
            for half in range(2):
                p2.append(hop_two(half, slot, e, other, dc))
                p2[-1].start()
        if core == 0:
            for half in range(2):
                p2.append(hop_two(half, slot, 1, 0, 1))
                p2[-1].start()

    def pack_slot(slot):
        for half in range(2):
            for e in range(8):
                pack(first.at[half, slot - 1, e], half, disp_of(half, slot, e))

    def start_slot(slot):
        for half in range(2):
            p1[half, slot] = send(
                first.at[half, slot - 1, pl.ds(1, 7)], mid.at[half, slot],
                p1_send.at[half, slot], p1_recv.at[half, slot], hop(half, slot),
            )
            p1e[half, slot] = send(
                first.at[half, slot - 1, 0], rows.at[(half * 4 + slot) * 8],
                p1e_send.at[half, slot], p1e_recv.at[half, slot], hop(half, slot),
            )

    for j in range(8):
        loads[3 + j].wait()
    for half in range(2):
        for e in range(1, 8):
            pack(mid.at[half, 0, e - 1], half, disp_of(half, 0, e))
        pack(rows.at[half * 32], half, disp_of(half, 0, 0))
    forward(0, 0)
    forward(0, 1)
    for slot in SLOTS:
        pack_slot(slot)
        start_slot(slot)

    loads[11].wait()
    for k in range(4):
        baraw[k] = jnp.transpose(bg[:, k * TILE : (k + 1) * TILE], (1, 0))

    for copy in act_copies:
        copy.wait_recv()
    for copy in ba_copies:
        copy.wait_recv()
    lam[mz] = jnp.zeros((8, BLK), jnp.float32)
    lam_g[...] = jnp.zeros_like(lam_g)
    cross[...] = jnp.zeros_like(cross)

    def proj_a_step(step, carry):
        block = ra[pl.ds(step * 16, 16)].reshape(512, BLK)
        value = jnp.dot(block, basis[...].reshape(BLK, BLK), preferred_element_type=jnp.float32)
        lam[mz] += jnp.sum((value * value).reshape(64, 8, BLK), axis=0)
        value = value.astype(jnp.bfloat16)
        for y in range(2):
            dy = step * 2 + y
            for dx in range(4):
                for dc in range(2):
                    r = (y * 8 + dx * 2 + dc) * 32
                    e = 2 * step + dc if y == 0 else 4 + step + 2 * dc
                    proj[dx * 8 + e, mz] = value[r : r + SUB]
                    proj[(4 + dy) * 8 + SECOND.index((dx, dc)), mz] = value[r + SUB : r + 2 * SUB]
        return carry

    lax.fori_loop(0, 2, proj_a_step, 0)

    z_copies = {}

    def z_send_half(slot, half, owner, k, target):
        piece = proj.at[pl.ds((half * 4 + slot) * 8, 8), owner]
        z_copies[slot, k] = send(piece, piece, z_send.at[slot, k], z_recv.at[slot, k], target)

    def z_start(slot):
        z_send_half(slot, 0, mz, 0, zat(1))
        z_send_half(slot, 1, mz, 1, zat(3))
        z_send_half(slot, 1, mz, 2, zat(1))
        z_send_half(slot, 0, mz, 3, zat(3))

    def z_forward(slot):
        z_copies[slot, 0].wait_recv()
        z_send_half(slot, 0, (mz + 3) % NZ, 4, zat(1))
        z_copies[slot, 1].wait_recv()
        z_send_half(slot, 1, (mz + 1) % NZ, 5, zat(3))

    z_start(0)
    lam_copies = [send(lam.at[mz], lam.at[mz], lam_send.at[k], lam_recv.at[k], zat(dz)) for k, dz in enumerate(SLOTS)]
    z_start(1)
    z_forward(0)
    z_start(3)
    z_forward(1)
    z_start(2)

    def take_slot(slot):
        for half in range(2):
            p1[half, slot].wait_recv()
        forward(slot, 0)


    take_slot(1)
    z_forward(3)
    take_slot(3)
    take_slot(2)
    forward(1, 1)
    forward(3, 1)
    forward(2, 1)
    z_forward(2)
    for copies in (act_copies, ba_copies, lam_copies):
        for copy in copies:
            copy.wait_send()

    def arrived(half, slot, blocks):
        for e in blocks:
            if slot == 0 and e == 0:
                continue
            (p1e[half, slot] if e == 0 else hop_two(half, slot, e, *SECOND[e])).wait_recv()

    def project(block):
        value = lax.dot_general(
            baraw[pl.ds(0, 4)].reshape(BLK, BLK), block, (((1,), (1,)), ((), ())), preferred_element_type=jnp.float32
        )
        square = value * value
        part = square[:, 0:128]
        for k in range(1, block.shape[0] // 128):
            part += square[:, k * 128 : (k + 1) * 128]
        lam_g[...] += part
        return value.astype(jnp.bfloat16)

    def proj_g(slot, count):
        def step(half, carry):
            g = half * 4 + slot
            value = project(rows[pl.ds(g * 8, count)].reshape(count * HALF, BLK))
            graw[g, :, :, pl.ds(0, count * HALF)] = value.reshape(8, 128, count * HALF)
            return carry

        for half in range(2):
            arrived(half, slot, range(count))
        lax.fori_loop(0, 2, step, 0)

    def add_cross(slot, count):
        def step(i, carry):
            half, part = i // 2, i % 2
            g = half * 4 + slot
            right = proj[pl.ds(g * 8, count)].reshape(count * HALF, BLK)
            left = graw[g, pl.ds(part * 4, 4), :, pl.ds(0, count * HALF)].reshape(512, count * HALF)
            prows = pl.ds(pl.multiple_of(part * 512, 512), 512)
            cross[prows, :] += jnp.dot(left, right, preferred_element_type=jnp.float32)
            return carry

        lax.fori_loop(0, 4, step, 0)

    def z_arrived(slot):
        for k in range(2, 6):
            z_copies[slot, k].wait_recv()

    for slot in (0, 1, 3):
        proj_g(slot, 8)
        z_arrived(slot)
        add_cross(slot, 8)
    proj_g(2, 4)
    z_arrived(2)
    add_cross(2, 4)

    for half in range(2):
        arrived(half, 2, range(4, 8))
    starts = [(half * 4 + 2) * 8 + 4 for half in range(2)]
    last_a = jnp.concatenate([proj[b : b + 4].reshape(256, BLK) for b in starts], axis=0)
    last_g = project(jnp.concatenate([rows[b : b + 4].reshape(256, BLK) for b in starts], axis=0))

    for copy in lam_copies:
        copy.wait_recv()
    total = cnt_ref[0]
    for s in range(1, N_DP):
        total += cnt_ref[s]
    row_total = total.astype(jnp.float32)
    row_a = jnp.sum(lam[0] + lam[1] + lam[2] + lam[3], axis=0, keepdims=True) / row_total
    col_g = jnp.sum(lam_g[...], axis=1, keepdims=True) / row_total
    for part in range(2):
        prows = slice(part * 512, part * 512 + 512)
        value = cross[prows, :] + jnp.dot(last_g[prows], last_a, preferred_element_type=jnp.float32)
        scaled = (value / row_total) / (col_g[prows] * row_a + damping)
        baraw[4 + part * 2 : 6 + part * 2] = scaled.astype(jnp.bfloat16).reshape(2, 256, BLK)

    out_copies = []
    for part in range(4):
        prows, cols = pl.ds(part * COLS, COLS), pl.ds(part * COLS, COLS)
        right = jnp.dot(
            bg[prows, :], baraw[pl.ds(4, 4)].reshape(BLK, BLK), preferred_element_type=jnp.float32
        ).astype(jnp.bfloat16)
        sa[:, :, cols] = lax.dot_general(
            basis[...].reshape(BLK, BLK), right, (((1,), (1,)), ((), ())), preferred_element_type=jnp.float32
        ).astype(jnp.bfloat16).reshape(N_DP, 32, COLS)
        for disp in SPREAD:
            i, target = index_of(*disp), at(*disp)
            out_copies.append(
                send(
                    sa.at[target, :, cols], out_hbm.at[me, :, cols],
                    out_send.at[part, i], out_recv.at[part, i], (target, mz),
                )
            )
    own = pltpu.make_async_copy(sa.at[me], out_hbm.at[me], store_sem)
    own.start()
    for copies in (p1.values(), p1e.values(), z_copies.values(), p2):
        for copy in copies:
            copy.wait_send()
    own.wait()
    for copy in out_copies:
        copy.wait()


def order_kernel(own_ref, pieces_hbm, out_hbm, held, load_sem, store_sem):
    loads = [pltpu.make_async_copy(pieces_hbm.at[own_ref[u]], held.at[u], load_sem.at[u]) for u in range(N_DP)]
    for copy in loads:
        copy.start()
    stores = []
    for layer in range(8):
        for copy in loads[layer * 4 : layer * 4 + 4]:
            copy.wait()
        stores.append(pltpu.make_async_copy(held.at[pl.ds(layer * 4, 4)], out_hbm.at[layer], store_sem.at[layer]))
        stores[-1].start()
    for copy in stores:
        copy.wait()


def local(acts, grads_out, counts, owners, bases_a, bases_g):
    smem = pl.BlockSpec(memory_space=pltpu.SMEM)
    hbm = pl.BlockSpec(memory_space=pl.ANY)
    bf16, f32 = jnp.bfloat16, jnp.float32
    dma = pltpu.SemaphoreType.DMA
    pieces = pl.pallas_call(
        kernel,
        out_shape=jax.ShapeDtypeStruct((N_DP, 32, BLK), bf16),
        in_specs=[smem, smem, hbm, hbm, hbm, hbm],
        out_specs=hbm,
        scratch_shapes=[
            pltpu.VMEM((8, 8, 128, HCOL), bf16),
            pltpu.VMEM((8, 2, SUB, BLK), bf16),
            pltpu.VMEM((8, 256, BLK), bf16),
            pltpu.VMEM((BLK, BLK), bf16),
            pltpu.VMEM((2, 3, 8, HALF, BLK), bf16),
            pltpu.VMEM((2, 4, 7, HALF, BLK), bf16),
            pltpu.VMEM((64, HALF, BLK), bf16),
            pltpu.VMEM((N_DP, 32, BLK), bf16),
            pltpu.VMEM((N_DP, 32, BLK), bf16),
            pltpu.VMEM((64, NZ, SUB, BLK), bf16),
            pltpu.VMEM((NZ, 256, BLK), bf16),
            pltpu.VMEM((NZ, 8, BLK), f32),
            pltpu.VMEM((BLK, 128), f32),
            pltpu.VMEM((BLK, BLK), f32),
            pltpu.VMEM((HALF, BLK), bf16),
            pltpu.SMEM((N_DP,), jnp.int32),
            dma((12,)),
            dma((N_DP,)), dma((N_DP,)),
            dma((3,)), dma((3,)),
            dma((3,)), dma((3,)),
            dma((2, 4)), dma((2, 4)),
            dma((2, 4)), dma((2, 4)),
            dma((2, 4, 8)), dma((2, 4, 8)),
            dma((4, 6)), dma((4, 6)),
            dma((4, N_DP)), dma((4, N_DP)),
            dma,
        ],
        compiler_params=pltpu.CompilerParams(
            collective_id=0, has_side_effects=True, vmem_limit_bytes=63 * 1024 * 1024
        ),
        name="kfac",
    )(owners, counts, acts, grads_out, bases_a, bases_g.reshape(BLK, BLK))
    return pl.pallas_call(
        order_kernel,
        out_shape=jax.ShapeDtypeStruct((8, 4, 32, BLK), bf16),
        in_specs=[smem, hbm],
        out_specs=hbm,
        scratch_shapes=[pltpu.VMEM((N_DP, 32, BLK), bf16), dma((N_DP,)), dma((8,))],
        name="order",
    )(owners, pieces)


def solution(mesh):
    placed = (
        P(None, "dp", None),
        P(None, "dp", "mp"),
        P(),
        P(),
        P(None, "mp", None),
        P("mp", "dp", None, None),
    )
    return jax.shard_map(
        local, mesh=mesh, in_specs=placed, out_specs=P(None, "mp", "dp", None), check_vma=False
    )
```

```python
import functools

import jax
import jax.numpy as jnp
from jax import lax
from jax.experimental import pallas as pl
from jax.experimental.pallas import tpu as pltpu
from jax.sharding import PartitionSpec as P

MESH = pl.DeviceIdType.MESH
damping = 0.0001
BLK = 1024
TILE = 256
HCOL = 512
NY, NX, NC, NZ = 4, 4, 2, 4
N_DP = NY * NX * NC
HALF = 64
SUB = HALF // NZ

PAIRS = [(2, 2), (1, 3), (3, 1), (2, 0), (0, 2), (1, 1), (3, 3), (2, 1), (2, 3), (1, 2), (3, 2), (0, 1), (1, 0), (0, 3), (3, 0)]
SPREAD = [(dy, dx, dc) for dc in range(NC) for dy, dx in PAIRS] + [(0, 0, 1)]
SLOTS = (1, 3, 2)
SECOND = [(0, 0), (0, 1), (2, 0), (2, 1), (1, 0), (3, 0), (1, 1), (3, 1)]
COLS = 256


def kernel(
    own_ref, cnt_ref, acts_hbm, grads_hbm, ba_hbm, bg_hbm, out_hbm,
    graw, araw, baraw, bg, first, mid, rows, sa, ra, proj, basis, lam, lam_g, cross, mask, inv_ref,
    load_sem, act_send, act_recv, ba_send, ba_recv, lam_send, lam_recv,
    p1_send, p1_recv, p1e_send, p1e_recv, p2_send, p2_recv, z_send, z_recv, out_send, out_recv, store_sem,
):
    me, mz = lax.axis_index("dp"), lax.axis_index("mp")
    my, mx, mc = me // 8, (me // 2) % 4, me % 2

    def at(dy, dx, dc):
        return ((my + dy) % NY) * 8 + ((mx + dx) % NX) * 2 + (mc + dc) % NC

    def zat(dz):
        return (me, (mz + dz) % NZ)

    def send(src, dst, ssem, rsem, target):
        copy = pltpu.make_async_remote_copy(
            src_ref=src, dst_ref=dst, send_sem=ssem, recv_sem=rsem, device_id=target, device_id_type=MESH
        )
        copy.start()
        return copy

    barrier = pltpu.get_barrier_semaphore()
    peers = [(at(*d), mz) for d in SPREAD] + [zat(dz) for dz in (1, 2, 3)]
    for peer in peers:
        pl.semaphore_signal(barrier, inc=1, device_id=peer, device_id_type=MESH)

    loads = [
        pltpu.make_async_copy(acts_hbm.at[:, pl.ds(mz * SUB, SUB)], araw.at[:, 0], load_sem.at[0]),
        pltpu.make_async_copy(acts_hbm.at[:, pl.ds(HALF + mz * SUB, SUB)], araw.at[:, 1], load_sem.at[1]),
    ]
    loads.append(pltpu.make_async_copy(ba_hbm, baraw, load_sem.at[10]))
    for j in range(8):
        loads.append(
            pltpu.make_async_copy(grads_hbm.at[:, :, pl.ds(j * HCOL, HCOL)], graw.at[j], load_sem.at[2 + j])
        )
    loads.append(pltpu.make_async_copy(bg_hbm, bg, load_sem.at[11]))
    for copy in loads:
        copy.start()

    def invert(d, carry):
        unit = jnp.int32(0)
        for u in range(1, N_DP):
            unit = jnp.where(own_ref[u] == d, u, unit)
        inv_ref[d] = unit
        return carry

    lax.fori_loop(0, N_DP, invert, 0)

    live = cnt_ref[me] - HALF
    row_ids = lax.broadcasted_iota(jnp.int32, (HALF, BLK), 0)
    mask[...] = jnp.where(row_ids < live, 1.0, 0.0).astype(jnp.bfloat16)

    sub_mask = mask[pl.ds(pl.multiple_of(mz * SUB, SUB), SUB), :]

    def pack_acts(dst, index, disp):
        layer = inv_ref[at(*disp)] // 4
        dst[index, pl.ds(0, SUB), :] = araw[layer, 0]
        dst[index, pl.ds(SUB, SUB), :] = araw[layer, 1] * sub_mask

    def index_of(dy, dx, dc):
        return (dy * 4 + dx) * 2 + dc

    loads[0].wait()
    loads[1].wait()
    for disp in SPREAD:
        pack_acts(sa, index_of(*disp), disp)
    pack_acts(ra, 0, (0, 0, 0))

    pl.semaphore_wait(barrier, len(peers))
    act_copies = []
    for disp in SPREAD:
        i = index_of(*disp)
        act_copies.append(send(sa.at[i], ra.at[i], act_send.at[i], act_recv.at[i], (at(*disp), mz)))

    loads[2].wait()
    basis[mz] = baraw[inv_ref[me] // 4]
    ba_copies = [
        send(basis.at[mz], basis.at[mz], ba_send.at[k], ba_recv.at[k], zat(dz)) for k, dz in enumerate(SLOTS)
    ]

    def disp_of(half, slot, e):
        other, dc = SECOND[e]
        return (other, slot, dc) if half == 0 else (slot, other, dc)

    def hop(half, slot):
        return (at(0, slot, 0) if half == 0 else at(slot, 0, 0), mz)

    def pack(dst, half, disp):
        unit = inv_ref[at(*disp)]
        layer, column = unit // 4, unit % 4
        for c in range(2):
            cols = pl.ds(c * HCOL, HCOL)
            block = graw[column * 2 + c, layer, pl.ds(half * HALF, HALF), :]
            dst[:, cols] = block if half == 0 else block * mask[:, cols]

    p1, p1e = {}, {}

    p2 = []

    def hop_two(half, slot, e, other, dc):
        return pltpu.make_async_remote_copy(
            src_ref=mid.at[half, slot, e - 1],
            dst_ref=rows.at[(half * 4 + slot) * 8 + e],
            send_sem=p2_send.at[half, slot, e],
            recv_sem=p2_recv.at[half, slot, e],
            device_id=(at(other, 0, dc) if half == 0 else at(0, other, dc), mz),
            device_id_type=MESH,
        )

    def forward(slot, core):
        dc = (core + mc) % 2
        for other in (2, 1, 3):
            e = jnp.where(dc == 0, SECOND.index((other, 0)), SECOND.index((other, 1)))
            for half in range(2):
                p2.append(hop_two(half, slot, e, other, dc))
                p2[-1].start()
        if core == 0:
            for half in range(2):
                p2.append(hop_two(half, slot, 1, 0, 1))
                p2[-1].start()

    def pack_slot(slot):
        for half in range(2):
            for e in range(8):
                pack(first.at[half, slot - 1, e], half, disp_of(half, slot, e))

    def start_slot(slot):
        for half in range(2):
            p1[half, slot] = send(
                first.at[half, slot - 1, pl.ds(1, 7)], mid.at[half, slot],
                p1_send.at[half, slot], p1_recv.at[half, slot], hop(half, slot),
            )
            p1e[half, slot] = send(
                first.at[half, slot - 1, 0], rows.at[(half * 4 + slot) * 8],
                p1e_send.at[half, slot], p1e_recv.at[half, slot], hop(half, slot),
            )

    for j in range(8):
        loads[3 + j].wait()
    for half in range(2):
        for e in range(1, 8):
            pack(mid.at[half, 0, e - 1], half, disp_of(half, 0, e))
        pack(rows.at[half * 32], half, disp_of(half, 0, 0))
    forward(0, 0)
    for slot in SLOTS:
        pack_slot(slot)
        start_slot(slot)
    forward(0, 1)

    loads[11].wait()
    for k in range(4):
        baraw[k] = jnp.transpose(bg[:, k * TILE : (k + 1) * TILE], (1, 0))

    for copy in act_copies:
        copy.wait_recv()
    for copy in ba_copies:
        copy.wait_recv()
    lam[mz] = jnp.zeros((8, BLK), jnp.float32)
    lam_g[...] = jnp.zeros_like(lam_g)
    cross[...] = jnp.zeros_like(cross)

    def proj_a_step(step, carry):
        block = ra[pl.ds(step * 16, 16)].reshape(512, BLK)
        value = jnp.dot(block, basis[...].reshape(BLK, BLK), preferred_element_type=jnp.float32)
        lam[mz] += jnp.sum((value * value).reshape(64, 8, BLK), axis=0)
        value = value.astype(jnp.bfloat16)
        for y in range(2):
            dy = step * 2 + y
            for dx in range(4):
                for dc in range(2):
                    r = (y * 8 + dx * 2 + dc) * 32
                    e = 2 * step + dc if y == 0 else 4 + step + 2 * dc
                    proj[dx * 8 + e, mz] = value[r : r + SUB]
                    proj[(4 + dy) * 8 + SECOND.index((dx, dc)), mz] = value[r + SUB : r + 2 * SUB]
        return carry

    lax.fori_loop(0, 2, proj_a_step, 0)

    z_copies = {}

    def z_send_half(slot, half, owner, k, target):
        piece = proj.at[pl.ds((half * 4 + slot) * 8, 8), owner]
        z_copies[slot, k] = send(piece, piece, z_send.at[slot, k], z_recv.at[slot, k], target)

    def z_start(slot):
        z_send_half(slot, 0, mz, 0, zat(1))
        z_send_half(slot, 1, mz, 1, zat(3))
        z_send_half(slot, 1, mz, 2, zat(1))
        z_send_half(slot, 0, mz, 3, zat(3))

    def z_forward(slot):
        z_copies[slot, 0].wait_recv()
        z_send_half(slot, 0, (mz + 3) % NZ, 4, zat(1))
        z_copies[slot, 1].wait_recv()
        z_send_half(slot, 1, (mz + 1) % NZ, 5, zat(3))

    z_start(0)
    lam_copies = [send(lam.at[mz], lam.at[mz], lam_send.at[k], lam_recv.at[k], zat(dz)) for k, dz in enumerate(SLOTS)]
    z_start(1)
    z_forward(0)
    z_start(3)
    z_forward(1)
    z_start(2)

    def take_slot(slot):
        for half in range(2):
            p1[half, slot].wait_recv()
        forward(slot, 0)


    take_slot(1)
    z_forward(3)
    take_slot(3)
    take_slot(2)
    forward(1, 1)
    forward(3, 1)
    forward(2, 1)
    z_forward(2)
    for copies in (act_copies, ba_copies, lam_copies):
        for copy in copies:
            copy.wait_send()

    def arrived(half, slot, blocks):
        for e in blocks:
            if slot == 0 and e == 0:
                continue
            (p1e[half, slot] if e == 0 else hop_two(half, slot, e, *SECOND[e])).wait_recv()

    def project(block):
        value = lax.dot_general(
            baraw[pl.ds(0, 4)].reshape(BLK, BLK), block, (((1,), (1,)), ((), ())), preferred_element_type=jnp.float32
        )
        square = value * value
        part = square[:, 0:128]
        for k in range(1, block.shape[0] // 128):
            part += square[:, k * 128 : (k + 1) * 128]
        lam_g[...] += part
        return value.astype(jnp.bfloat16)

    def proj_g(slot, count):
        def step(half, carry):
            g = half * 4 + slot
            value = project(rows[pl.ds(g * 8, count)].reshape(count * HALF, BLK))
            graw[g, :, :, pl.ds(0, count * HALF)] = value.reshape(8, 128, count * HALF)
            return carry

        for half in range(2):
            arrived(half, slot, range(count))
        lax.fori_loop(0, 2, step, 0)

    def add_cross(slot, count):
        def step(i, carry):
            half, part = i // 2, i % 2
            g = half * 4 + slot
            right = proj[pl.ds(g * 8, count)].reshape(count * HALF, BLK)
            left = graw[g, pl.ds(part * 4, 4), :, pl.ds(0, count * HALF)].reshape(512, count * HALF)
            prows = pl.ds(pl.multiple_of(part * 512, 512), 512)
            cross[prows, :] += jnp.dot(left, right, preferred_element_type=jnp.float32)
            return carry

        lax.fori_loop(0, 4, step, 0)

    def z_arrived(slot):
        for k in range(2, 6):
            z_copies[slot, k].wait_recv()

    for slot in (0, 1, 3):
        proj_g(slot, 8)
        z_arrived(slot)
        add_cross(slot, 8)
    for copy in lam_copies:
        copy.wait_recv()
    total = cnt_ref[0]
    for s in range(1, N_DP):
        total += cnt_ref[s]
    row_total = total.astype(jnp.float32)
    row_a = jnp.sum(lam[0] + lam[1] + lam[2] + lam[3], axis=0, keepdims=True) / row_total
    proj_g(2, 4)
    z_arrived(2)
    add_cross(2, 4)

    for half in range(2):
        arrived(half, 2, range(4, 8))
    starts = [(half * 4 + 2) * 8 + 4 for half in range(2)]
    last_a = jnp.concatenate([proj[b : b + 4].reshape(256, BLK) for b in starts], axis=0)
    last_g = project(jnp.concatenate([rows[b : b + 4].reshape(256, BLK) for b in starts], axis=0))

    col_g = jnp.sum(lam_g[...], axis=1, keepdims=True) / row_total
    for part in range(2):
        prows = slice(part * 512, part * 512 + 512)
        value = cross[prows, :] + jnp.dot(last_g[prows], last_a, preferred_element_type=jnp.float32)
        scaled = (value / row_total) / (col_g[prows] * row_a + damping)
        baraw[4 + part * 2 : 6 + part * 2] = scaled.astype(jnp.bfloat16).reshape(2, 256, BLK)

    out_copies = []
    for part in range(4):
        prows, cols = pl.ds(part * COLS, COLS), pl.ds(part * COLS, COLS)
        right = jnp.dot(
            bg[prows, :], baraw[pl.ds(4, 4)].reshape(BLK, BLK), preferred_element_type=jnp.float32
        ).astype(jnp.bfloat16)
        sa[:, :, cols] = lax.dot_general(
            basis[...].reshape(BLK, BLK), right, (((1,), (1,)), ((), ())), preferred_element_type=jnp.float32
        ).astype(jnp.bfloat16).reshape(N_DP, 32, COLS)
        for disp in SPREAD:
            i, target = index_of(*disp), at(*disp)
            out_copies.append(
                send(
                    sa.at[target, :, cols], out_hbm.at[me, :, cols],
                    out_send.at[part, i], out_recv.at[part, i], (target, mz),
                )
            )
    own = pltpu.make_async_copy(sa.at[me], out_hbm.at[me], store_sem)
    own.start()
    for copies in (p1.values(), p1e.values(), z_copies.values(), p2):
        for copy in copies:
            copy.wait_send()
    own.wait()
    for copy in out_copies:
        copy.wait()


def order_kernel(own_ref, pieces_hbm, out_hbm, held, load_sem, store_sem):
    loads = [pltpu.make_async_copy(pieces_hbm.at[own_ref[u]], held.at[u], load_sem.at[u]) for u in range(N_DP)]
    for copy in loads:
        copy.start()
    stores = []
    for layer in range(8):
        for copy in loads[layer * 4 : layer * 4 + 4]:
            copy.wait()
        stores.append(pltpu.make_async_copy(held.at[pl.ds(layer * 4, 4)], out_hbm.at[layer], store_sem.at[layer]))
        stores[-1].start()
    for copy in stores:
        copy.wait()


def local(acts, grads_out, counts, owners, bases_a, bases_g):
    smem = pl.BlockSpec(memory_space=pltpu.SMEM)
    hbm = pl.BlockSpec(memory_space=pl.ANY)
    bf16, f32 = jnp.bfloat16, jnp.float32
    dma = pltpu.SemaphoreType.DMA
    pieces = pl.pallas_call(
        kernel,
        out_shape=jax.ShapeDtypeStruct((N_DP, 32, BLK), bf16),
        in_specs=[smem, smem, hbm, hbm, hbm, hbm],
        out_specs=hbm,
        scratch_shapes=[
            pltpu.VMEM((8, 8, 128, HCOL), bf16),
            pltpu.VMEM((8, 2, SUB, BLK), bf16),
            pltpu.VMEM((8, 256, BLK), bf16),
            pltpu.VMEM((BLK, BLK), bf16),
            pltpu.VMEM((2, 3, 8, HALF, BLK), bf16),
            pltpu.VMEM((2, 4, 7, HALF, BLK), bf16),
            pltpu.VMEM((64, HALF, BLK), bf16),
            pltpu.VMEM((N_DP, 32, BLK), bf16),
            pltpu.VMEM((N_DP, 32, BLK), bf16),
            pltpu.VMEM((64, NZ, SUB, BLK), bf16),
            pltpu.VMEM((NZ, 256, BLK), bf16),
            pltpu.VMEM((NZ, 8, BLK), f32),
            pltpu.VMEM((BLK, 128), f32),
            pltpu.VMEM((BLK, BLK), f32),
            pltpu.VMEM((HALF, BLK), bf16),
            pltpu.SMEM((N_DP,), jnp.int32),
            dma((12,)),
            dma((N_DP,)), dma((N_DP,)),
            dma((3,)), dma((3,)),
            dma((3,)), dma((3,)),
            dma((2, 4)), dma((2, 4)),
            dma((2, 4)), dma((2, 4)),
            dma((2, 4, 8)), dma((2, 4, 8)),
            dma((4, 6)), dma((4, 6)),
            dma((4, N_DP)), dma((4, N_DP)),
            dma,
        ],
        compiler_params=pltpu.CompilerParams(
            collective_id=0, has_side_effects=True, vmem_limit_bytes=63 * 1024 * 1024
        ),
        name="kfac",
    )(owners, counts, acts, grads_out, bases_a, bases_g.reshape(BLK, BLK))
    return pl.pallas_call(
        order_kernel,
        out_shape=jax.ShapeDtypeStruct((8, 4, 32, BLK), bf16),
        in_specs=[smem, hbm],
        out_specs=hbm,
        scratch_shapes=[pltpu.VMEM((N_DP, 32, BLK), bf16), dma((N_DP,)), dma((8,))],
        name="order",
    )(owners, pieces)


def solution(mesh):
    placed = (
        P(None, "dp", None),
        P(None, "dp", "mp"),
        P(),
        P(),
        P(None, "mp", None),
        P("mp", "dp", None, None),
    )
    return jax.shard_map(
        local, mesh=mesh, in_specs=placed, out_specs=P(None, "mp", "dp", None), check_vma=False
    )
```
